32 devices in a mesh: groups: 2 (over y), tile: 4 (over z), dither: 2 (over x), band: 2 (over core).
Axes of the slice: x: 2, y: 2, z: 4, core: 2. Of those that a mesh axis runs over, the one named last changes fastest.
Arguments:
- spectra: bfloat16 [2048, 1024], P(('groups', 'tile'), 'band'), parts along dimension 0, may hold values from -6 to 6
- psf_blocks: bfloat16 [16, 128, 128], replicated, may hold values from -0.5 to 0.5
- observed: bfloat16 [4, 4096, 128], P(('groups', 'dither'), 'tile'), parts along dimension 0, may hold values from -6 to 6
- bad_mask: int32 [4, 4096, 128], P(('groups', 'dither'), 'tile'), parts along dimension 0, may hold values 0 or 1
- trace_tile: int32 [32768, 1], P(('groups', 'tile', 'dither', 'band')), parts along dimension 0, may hold values from 0 to 3; in each aligned block of 1024 rows (0 to 1023, 1024 to 2047, ...) at most 512 rows name the same one
- trace_slot: int32 [32768], P(('groups', 'tile', 'dither', 'band')), parts along dimension 0, may hold values from 0 to 1023
- trace_source: int32 [32768, 1], P(('groups', 'tile', 'dither', 'band')), parts along dimension 0, may hold values from 0 to 255; in each aligned block of 1024 rows (0 to 1023, 1024 to 2047, ...) at most 8 rows name the same one
- trace_block: int32 [32768], P(('groups', 'tile', 'dither', 'band')), parts along dimension 0, may hold values from 0 to 3
- psf_index: int32 [32768], P(('groups', 'tile', 'dither', 'band')), parts along dimension 0, may hold values from 0 to 15
Outputs:
- gradient: float32 [2048, 1024], P(('groups', 'tile', 'dither'), 'band'), parts along dimension 0
- residual: bfloat16 [4, 4096, 128], P(('groups', 'dither'), 'tile'), parts along dimension 0
The draws below stay inside these ranges and needn't reach their ends.
There are 2 independent parts, one for each index of `groups`. The reference program is written for one: setup_inputs(seed, part) draws one part's arguments, and reference() takes and returns one part's arrays. A program takes and returns all parts, laid end to end along the dimension named above; an argument that names none is the same for every part. Nothing has to cross between parts.
Inputs may be any that keep to these rules, and one draw needn't show every extreme that they name: `trace_tile`: among the trace blocks of one sky region, dither and wavelength half, at most 512 name the same tile, and in every draw some tile is named by exactly 512 of them for some such group. `trace_source`: among the trace blocks of one sky region, dither and wavelength half, at most 8 name the same source, and in every draw some source is named by exactly 8 of them for some such group.
All inputs are finite; a program needn't handle non-finite values. No bound on the sum of `bad_mask` on one device may be relied on, other than what follows from the above.
Results may differ from the reference program's by a relative error of at most 0.006.
Values may be sent and summed in bfloat16 or wider, within the bound.
A program may use at most 64 MiB of HBM per device.

```python
import math
import jax
import jax.numpy as jnp
import numpy as np
from jax import lax

BIN = 128
TRACE = 128
NWAVE = 1024
NPSF = 16
SRC_DEV = 256
ENT_DEV = 1024
SLOTS = 1024
NWB = 8
WB_DEV = 4
TILES = 4
DITHERS = 2
BANDS = 2
SOURCES = 1024
ENTRIES = 16384
CAP = 512
SRC_MOST = 8
N_TILE = 4


def set_ends(values, stream_key, smallest, top_value):
    place = [jax.random.randint(jax.random.fold_in(stream_key, axis), (), 0, length) for axis, length in enumerate(values.shape)]
    longest = values.shape.index(max(values.shape))
    beside = place[:longest] + [(place[longest] + 1) % values.shape[longest]] + place[longest + 1:]
    return values.at[tuple(place)].set(smallest).at[tuple(beside)].set(top_value)


def levels(own_key, extent, cuts, smallest, largest):
    gain = 1.0
    for dim, shards_of in cuts:
        steps = jax.random.uniform(jax.random.fold_in(jax.random.fold_in(own_key, 6), dim), (shards_of,), jnp.float32, smallest / len(cuts), largest / len(cuts))
        gain = gain * jnp.repeat(jnp.exp(steps), extent[dim] // shards_of).reshape((-1,) + (1,) * (len(extent) - 1 - dim))
    return gain


def deal_out(own_key, own, number, rows, count, top, bound, slope):
    sequence = jax.random.permutation(own_key, count)
    packed, usual = portions_of(count, rows * top, bound, slope, True), portions_of(count, rows * top, bound, slope, False)
    places = jnp.arange(count)

    def named(lengths, turn):
        used = int((lengths > 0).sum())
        fixed = max(1, used // 4)
        moved = fixed + (places - fixed + turn * (used - fixed)) % max(1, count - fixed)
        return jnp.zeros((count,), jnp.int32).at[sequence[jnp.where(places < fixed, places, moved)]].set(jnp.asarray(lengths, jnp.int32))

    lengths = jnp.where(number % 4 == 0, named(packed, number // 4), named(usual, number - number // 4 - 1))
    mixed = jax.random.permutation(jax.random.fold_in(own, 3), count)
    source_of, receiver = mixed[0:count // 2 * 2:2], mixed[1:count // 2 * 2:2]
    slack = jnp.minimum(lengths[source_of] - 1, bound - lengths[receiver]) // 2
    slack = jnp.where((source_of == sequence[0]) | (receiver == sequence[0]) | (lengths[receiver] == 0), 0, jnp.maximum(slack, 0))
    moved = jax.random.randint(jax.random.fold_in(own, 4), (count // 2,), 0, 1 << 20) % (slack + 1)
    lengths = lengths.at[source_of].add(-moved).at[receiver].add(moved)
    members = jnp.searchsorted(jnp.cumsum(lengths), jnp.arange(rows * top), side="right").astype(jnp.int32)
    table = members.reshape(top, rows).T
    table = table[jax.random.permutation(jax.random.fold_in(own, 1), rows)]
    turn = jax.random.randint(jax.random.fold_in(own, 2), (rows, 1), 0, top)
    return jnp.take_along_axis(table, (jnp.arange(top)[None, :] + turn) % top, axis=1)


def portions_of(amount, total, limit, slope, full):
    portions = [(1 << 20) // math.isqrt(grade ** slope) + 1 for grade in range(1, amount + 1)]
    largest = limit if full else min(limit, max(-(-total // amount), total * portions[0] // sum(portions)))
    least = 1 if total - largest >= amount - 1 else 0
    holding, rest = [largest] + [least] * (amount - 1), total - largest - least * (amount - 1)
    while rest > 0:
        candidates = [i for i in range(1, amount) if holding[i] < largest] or [i for i in range(1, amount) if holding[i] < limit]
        whole, budget = sum([portions[i] for i in candidates]), rest
        for i in candidates:
            addition = min(limit - holding[i], max(1, budget * portions[i] // whole), rest)
            holding[i] = holding[i] + addition
            rest = rest - addition
    return np.array(holding)


def centred(own_key, dims, deviation, bound, split=(), kind=jnp.bfloat16):
    array = deviation * jax.random.normal(own_key, dims, jnp.float32)
    if split:
        array = array * levels(own_key, dims, split, -0.22, 0.18)
    return jnp.clip(array, -bound, bound).astype(kind)


def setup_inputs(seed: int = 0, part: int = 0) -> dict:
    keys = jax.random.split(jax.random.key(seed), 10)
    part_keys = jax.random.split(jax.random.fold_in(keys[9], part), 10)
    spectra = centred(part_keys[0], (SOURCES, NWAVE), 1.0, 6.0, ((0, 4), (1, 2)))
    psf_blocks = centred(keys[1], (NPSF, BIN, TRACE), BIN ** -0.5, 0.5)
    observed = centred(part_keys[2], (DITHERS, TILES * SLOTS, TRACE), 1.0, 6.0, ((0, 2), (1, 4)))
    bad_mask = set_ends((jax.random.randint(part_keys[3], (DITHERS, TILES * SLOTS, TRACE), 0, 8) < 7).astype(jnp.int32), jax.random.fold_in(part_keys[3], 1), 0, 1)
    trace_tile_keys = jax.random.split(jax.random.fold_in(part_keys[4], 1), ENTRIES // ENT_DEV)
    trace_tile_turns = jax.random.permutation(jax.random.fold_in(part_keys[4], 3), ENTRIES // ENT_DEV)
    trace_tile = jax.vmap(lambda own, number: deal_out(jax.random.fold_in(part_keys[4], 2), own, number, ENT_DEV, N_TILE, 1, CAP, 2))(trace_tile_keys, trace_tile_turns).reshape((ENTRIES, 1))
    trace_slot = set_ends(jax.random.randint(part_keys[5], (ENTRIES,), 0, SLOTS), jax.random.fold_in(part_keys[5], 1), 0, SLOTS - 1).astype(jnp.int32)
    trace_source_keys = jax.random.split(jax.random.fold_in(part_keys[6], 1), ENTRIES // ENT_DEV)
    trace_source_turns = jax.random.permutation(jax.random.fold_in(part_keys[6], 3), ENTRIES // ENT_DEV)
    trace_source = jax.vmap(lambda own, number: deal_out(jax.random.fold_in(part_keys[6], 2), own, number, ENT_DEV, SRC_DEV, 1, SRC_MOST, 1))(trace_source_keys, trace_source_turns).reshape((ENTRIES, 1))
    trace_block = set_ends(jax.random.randint(part_keys[7], (ENTRIES,), 0, WB_DEV), jax.random.fold_in(part_keys[7], 1), 0, WB_DEV - 1).astype(jnp.int32)
    psf_index = set_ends(jax.random.randint(part_keys[8], (ENTRIES,), 0, NPSF), jax.random.fold_in(part_keys[8], 1), 0, NPSF - 1).astype(jnp.int32)
    return {"spectra": spectra, "psf_blocks": psf_blocks, "observed": observed, "bad_mask": bad_mask, "trace_tile": trace_tile, "trace_slot": trace_slot, "trace_source": trace_source, "trace_block": trace_block, "psf_index": psf_index}


def reference(spectra, psf_blocks, observed, bad_mask, trace_tile, trace_slot, trace_source, trace_block, psf_index):
    entry_index = jnp.arange(ENTRIES, dtype=jnp.int32)
    device = entry_index // ENT_DEV
    region = device // (DITHERS * BANDS)
    dither = (device // BANDS) % DITHERS
    band_index = device % BANDS
    source = region * SRC_DEV + trace_source[:, 0].astype(jnp.int32)
    spec_block = band_index * WB_DEV + trace_block.astype(jnp.int32)
    pixel_rows = ((dither * TILES + trace_tile[:, 0].astype(jnp.int32)) * SLOTS + trace_slot.astype(jnp.int32)).astype(jnp.int32)
    spec_rows = (source * NWB + spec_block).astype(jnp.int32)
    stacked = spectra.reshape(SOURCES * NWB, BIN)
    batch_size = math.gcd(ENTRIES, 1024)

    def forward(inputs):
        rows, kinds = inputs
        values = stacked[rows].astype(jnp.float32)
        matrices = psf_blocks[kinds].astype(jnp.float32)
        return jnp.einsum("ek,ekj->ej", values, matrices).astype(jnp.bfloat16)

    traces = lax.map(forward, (spec_rows.reshape(-1, batch_size), psf_index.reshape(-1, batch_size)))
    traces = traces.reshape(ENTRIES, TRACE)
    model_image = jax.ops.segment_sum(traces.astype(jnp.float32), pixel_rows, DITHERS * TILES * SLOTS)
    masks = bad_mask.reshape(-1, TRACE).astype(jnp.float32)
    residual = (masks * (model_image - observed.reshape(-1, TRACE).astype(jnp.float32))).astype(jnp.bfloat16)

    def backward(inputs):
        rows, kinds = inputs
        rows_res = residual[rows].astype(jnp.float32)
        matrices = psf_blocks[kinds].astype(jnp.float32)
        return jnp.einsum("ej,ekj->ek", rows_res, matrices)

    grad_terms = lax.map(backward, (pixel_rows.reshape(-1, batch_size), psf_index.reshape(-1, batch_size)))
    grad_terms = grad_terms.reshape(ENTRIES, BIN)
    gradient = jax.ops.segment_sum(grad_terms, spec_rows, SOURCES * NWB).reshape(SOURCES, NWAVE)
    return gradient, residual.reshape(DITHERS, TILES * SLOTS, TRACE)
```

```python
import functools

import jax
import jax.numpy as jnp
from jax import lax
from jax.experimental import pallas as pl
from jax.experimental.pallas import tpu as pltpu
from jax.sharding import PartitionSpec as P

MESH = pl.DeviceIdType.MESH
F32, BF16 = jnp.float32, jnp.bfloat16


def dot(a, b):
    return jnp.dot(a, b, preferred_element_type=F32)


def kernel(
    cfg,
    spectra_ref, psf_ref, obs_ref, bad_ref, tile_ref, slot_ref, src_ref, blk_ref, kind_ref,
    grad_ref, res_ref,
    cols, traces, masked, onehot, onehot_t, psf_t, own, fsend, frecv, zrecv, zsend,
    resid, rows, terms, dsend, drecv,
    fs_sem, fr_sem, zs_sem, zr_sem, gs_sem, gr_sem, ps_sem, pr_sem, ds_sem, dr_sem,
):
    n, nd, parts, sub = cfg
    entries = tile_ref.shape[1]
    slots = obs_ref.shape[0]
    half = slots // 2
    kinds, bins, pixels = psf_ref.shape
    sources, wide = spectra_ref.shape
    blocks = wide // bins
    step_rows = min(256, entries)
    z = lax.axis_index("tile")
    b = lax.axis_index("band")
    d = lax.axis_index("dither")
    peer = {"band": 1 - b}
    above, below = {"tile": z + 1}, {"tile": z - 1}
    has_above, has_below = z < n - 1, z > 0

    barrier = pltpu.get_barrier_semaphore()

    def greet(where):
        pl.semaphore_signal(barrier, inc=1, device_id=where, device_id_type=MESH)

    greet(peer)
    pl.when(has_above)(lambda: greet(above))
    pl.when(has_below)(lambda: greet(below))
    for k in range(1, nd):
        greet({"dither": lax.rem(d + k, nd)})

    stack = [tile_ref[...], slot_ref[...], src_ref[...], blk_ref[...], kind_ref[...]]
    cols[...] = jnp.concatenate(stack + [kind_ref[...]] * 3, axis=0).T

    def spread(values, which, count):
        return jnp.concatenate(
            [jnp.where(which == k, values, 0.0).astype(BF16) for k in range(count)], axis=1
        )

    def forward(i, _):
        at = pl.ds(pl.multiple_of(i * step_rows, step_rows), step_rows)
        col = cols[at, :]
        lane = lax.broadcasted_iota(jnp.int32, (step_rows, sources), 1)
        pick = jnp.where(lane == col[:, 2:3], 1.0, 0.0).astype(BF16)
        found = dot(pick, spectra_ref[...])
        block = jnp.broadcast_to(col[:, 3:4], (step_rows, bins))
        value = jnp.zeros((step_rows, bins), F32)
        for k in range(blocks):
            value = jnp.where(block == k, found[:, k * bins:(k + 1) * bins], value)
        kind = jnp.broadcast_to(col[:, 4:5], (step_rows, bins))
        table = psf_ref[...].reshape(kinds * bins, pixels)
        traces[at, :] = dot(spread(value, kind, kinds), table).astype(BF16)
        return _

    lax.fori_loop(0, entries // step_rows, forward, 0)

    def mark(i, _):
        size = 128
        at = pl.ds(pl.multiple_of(i * size, size), size)
        row = lax.broadcasted_iota(jnp.int32, (size, entries), 0) + i * size
        onehot[at, :] = jnp.where(row == slot_ref[...], 1.0, 0.0).astype(BF16)
        return _

    lax.fori_loop(0, slots // 128, mark, 0)

    pl.semaphore_wait(barrier, 1 + (nd - 1) + has_above.astype(jnp.int32) + has_below.astype(jnp.int32))

    def my_rows(c):
        return pl.ds(pl.multiple_of(b * half + c * sub, sub), sub)

    def peer_rows(c):
        return pl.ds(pl.multiple_of((1 - b) * half + c * sub, sub), sub)

    def copy(src, dst, send, recv, where):
        return pltpu.make_async_remote_copy(
            src_ref=src, dst_ref=dst, send_sem=send, recv_sem=recv,
            device_id=where, device_id_type=MESH,
        )

    def f_copy(t, c):
        return copy(fsend.at[t, c], frecv.at[t, c], fs_sem.at[t, c], fr_sem.at[t, c], peer)

    def z_copy(way, t, c):
        return copy(
            zsend.at[t, c], zrecv.at[way, t, c], zs_sem.at[t, c], zr_sem.at[way, t, c],
            below if way else above,
        )

    def g_copy(way, t, c):
        block = resid.at[t, my_rows(c)]
        return copy(
            block, block, gs_sem.at[way, t, c], gr_sem.at[way, t, c], below if way else above
        )

    def p_copy(t, c, arriving=False):
        block = resid.at[t, peer_rows(c) if arriving else my_rows(c)]
        return copy(block, block, ps_sem.at[t, c], pr_sem.at[t, c], peer)

    def scatter(t, c):
        tile = jnp.broadcast_to(cols[:, 0:1], (entries, pixels))
        masked[...] = jnp.where(tile == t, traces[...].astype(F32), 0.0).astype(BF16)
        fsend[t, c] = dot(onehot[peer_rows(c), :], masked[...]).astype(BF16)
        f_copy(t, c).start()
        own[t, c] = dot(onehot[my_rows(c), :], masked[...])

    def up_tile(s):
        return n - 1 - s + z

    def down_tile(s):
        return s - (n - 1 - z)

    def both(s, act):
        pl.when(s >= z)(lambda: act(0, up_tile(s)))
        pl.when(s >= n - 1 - z)(lambda: act(1, down_tile(s)))

    def scatter_step(s, c):
        both(s, lambda way, t: scatter(t, c))

    def take(way, t, c):
        def go():
            z_copy(way, t, c).wait_recv()
            own[t, c] = own[t, c] + zrecv[way, t, c].astype(F32)

        pl.when(has_above if way else has_below)(go)

    def reduce_step(s, c):
        def act(way, t):
            f_copy(t, c).wait_recv()
            own[t, c] = own[t, c] + frecv[t, c].astype(F32)
            take(way, t, c)
            zsend[t, c] = own[t, c].astype(BF16)
            z_copy(way, t, c).start()

        both(s, act)

    def pass_on(way, t, c):
        pl.when(has_below if way else has_above)(lambda: g_copy(way, t, c).start())

    def finish(c):
        f_copy(z, c).wait_recv()
        own[z, c] = own[z, c] + frecv[z, c].astype(F32)
        take(0, z, c)
        take(1, z, c)
        at = my_rows(c)
        out = bad_ref[at, :].astype(F32) * (own[z, c] - obs_ref[at, :].astype(F32))
        resid[z, at, :] = out.astype(BF16)
        pass_on(0, z, c)
        pass_on(1, z, c)
        p_copy(z, c).start()

    def around(s, act):
        pl.when(z - s >= 0)(lambda: act(0, z - s))
        pl.when(z + s <= n - 1)(lambda: act(1, z + s))

    def gather_step(s, c):
        def act(way, t):
            g_copy(way, t, c).wait_recv()
            pass_on(way, t, c)
            p_copy(t, c).start()

        around(s, act)

    def use(t, c):
        p_copy(t, c, arriving=True).wait_recv()

        def block(i, _):
            at = pl.ds(pl.multiple_of(i * step_rows, step_rows), step_rows)
            got = dot(onehot_t[at, my_rows(c)], resid[t, my_rows(c), :])
            got = got + dot(onehot_t[at, peer_rows(c)], resid[t, peer_rows(c), :])
            tile = jnp.broadcast_to(cols[at, 0:1], (step_rows, pixels))
            rows[at, :] = rows[at, :] + jnp.where(tile == t, got, 0.0)
            return _

        lax.fori_loop(0, entries // step_rows, block, 0)

    def loop(first, last, act):
        def body(s, _):
            act(s)
            return _

        lax.fori_loop(first, last, body, 0)

    loop(0, n - 1, lambda s: scatter_step(s, 0))
    reduce_step(0, 0)
    scatter(z, 0)

    rows[...] = jnp.zeros_like(rows)

    def turn(k, _):
        at = pl.ds(pl.multiple_of(k * pixels, pixels), pixels)
        psf_t[at, :] = psf_ref[k].T
        return _

    lax.fori_loop(0, kinds, turn, 0)

    def mark_t(i, _):
        size = 128
        at = pl.ds(pl.multiple_of(i * size, size), size)
        lane = lax.broadcasted_iota(jnp.int32, (size, slots), 1)
        onehot_t[at, :] = jnp.where(lane == cols[at, 1:2], 1.0, 0.0).astype(BF16)
        return _

    lax.fori_loop(0, entries // 128, mark_t, 0)

    def phase_first(s):
        reduce_step(s, 0)
        if parts > 1:
            scatter_step(s - 1, 1)

    loop(1, n - 1, phase_first)
    if parts > 1:
        scatter_step(n - 2, 1)
        scatter(z, 1)
    finish(0)

    for c in range(1, parts + 1):
        reducing = c < parts

        def phase(s):
            if reducing:
                reduce_step(s - 1, c)
            gather_step(s, c - 1)

            def earlier():
                if reducing and c + 1 < parts:
                    scatter_step(s - 1, c + 1)

            earlier()
            pl.when(s == 1)(lambda: use(z, c - 1))
            pl.when(s > 1)(lambda: around(s - 1, lambda way, t: use(t, c - 1)))

        loop(1, n, phase)
        if reducing:
            if c + 1 < parts:
                scatter(z, c + 1)
            finish(c)
        around(n - 1, lambda way, t: use(t, c - 1))

    res_ref[...] = resid[z]

    def backward(i, _):
        at = pl.ds(pl.multiple_of(i * step_rows, step_rows), step_rows)
        col = cols[at, :]
        kind = jnp.broadcast_to(col[:, 4:5], (step_rows, pixels))
        term = dot(spread(rows[at, :], kind, kinds), psf_t[...])
        block = jnp.broadcast_to(col[:, 3:4], (step_rows, bins))
        terms[at, :] = spread(term, block, blocks)
        return _

    lax.fori_loop(0, entries // step_rows, backward, 0)

    share = sources // nd

    def summed(to):
        row = lax.broadcasted_iota(jnp.int32, (share, entries), 0) + to * share
        member = jnp.where(row == src_ref[...], 1.0, 0.0).astype(BF16)
        return dot(member, terms[...])

    def d_copy(k):
        to = lax.rem(d + k, nd)
        return copy(
            dsend.at[k - 1], drecv.at[k - 1], ds_sem.at[k - 1], dr_sem.at[k - 1], {"dither": to}
        )

    for k in range(1, nd):
        dsend[k - 1] = summed(lax.rem(d + k, nd)).astype(BF16)
        d_copy(k).start()
    grad_ref[...] = summed(d)
    for k in range(1, nd):
        d_copy(k).wait_recv()
        grad_ref[...] = grad_ref[...] + drecv[k - 1].astype(F32)
        d_copy(k).wait_send()

    for c in range(parts):
        loop(0, n, lambda t: f_copy(t, c).wait_send())
        loop(0, n - 1, lambda s: both(s, lambda way, t: z_copy(way, t, c).wait_send()))

        def sent(way, t):
            pl.when(has_below if way else has_above)(lambda: g_copy(way, t, c).wait_send())

        sent(0, z)
        sent(1, z)
        loop(1, n, lambda s: around(s, sent))
        loop(0, n, lambda t: p_copy(t, c).wait_send())


def per_device(
    n, nd, spectra, psf_blocks, observed, bad_mask,
    trace_tile, trace_slot, trace_source, trace_block, psf_index,
):
    entries = trace_slot.shape[0]
    slots, pixels = observed.shape[1:]
    kinds, bins, _ = psf_blocks.shape
    sources, wide = spectra.shape
    parts = 2
    sub = slots // 2 // parts
    row = lambda a: a.reshape(1, entries)
    dma = pltpu.SemaphoreType.DMA
    grad, res = pl.pallas_call(
        functools.partial(kernel, (n, nd, parts, sub)),
        out_shape=(
            jax.ShapeDtypeStruct((sources // nd, wide), F32),
            jax.ShapeDtypeStruct((slots, pixels), BF16),
        ),
        in_specs=[pl.BlockSpec(memory_space=pltpu.VMEM)] * 9,
        out_specs=[pl.BlockSpec(memory_space=pltpu.VMEM)] * 2,
        scratch_shapes=[
            pltpu.VMEM((entries, 8), jnp.int32),
            pltpu.VMEM((entries, pixels), BF16),
            pltpu.VMEM((entries, pixels), BF16),
            pltpu.VMEM((slots, entries), BF16),
            pltpu.VMEM((entries, slots), BF16),
            pltpu.VMEM((kinds * pixels, bins), BF16),
            pltpu.VMEM((n, parts, sub, pixels), F32),
            pltpu.VMEM((n, parts, sub, pixels), BF16),
            pltpu.VMEM((n, parts, sub, pixels), BF16),
            pltpu.VMEM((2, n, parts, sub, pixels), BF16),
            pltpu.VMEM((n, parts, sub, pixels), BF16),
            pltpu.VMEM((n, slots, pixels), BF16),
            pltpu.VMEM((entries, pixels), F32),
            pltpu.VMEM((entries, wide), BF16),
            pltpu.VMEM((nd - 1, sources // nd, wide), BF16),
            pltpu.VMEM((nd - 1, sources // nd, wide), BF16),
            dma((n, parts)), dma((n, parts)),
            dma((n, parts)), dma((2, n, parts)),
            dma((2, n, parts)), dma((2, n, parts)),
            dma((n, parts)), dma((n, parts)),
            dma((nd - 1,)), dma((nd - 1,)),
        ],
        compiler_params=pltpu.CompilerParams(
            collective_id=0, has_side_effects=True, vmem_limit_bytes=56 * 1024 * 1024
        ),
        cost_estimate=pl.CostEstimate(
            flops=2 * entries * pixels * (2 * kinds * bins + 2 * n * slots + 8 * sources),
            bytes_accessed=2 * 1024 * 1024,
            transcendentals=0,
        ),
    )(
        spectra, psf_blocks, observed[0], bad_mask[0],
        row(trace_tile), row(trace_slot), row(trace_source), row(trace_block), row(psf_index),
    )
    return grad, res[None]


def solution(mesh):
    in_specs = (
        P(("groups", "tile"), "band"),
        P(),
        P(("groups", "dither"), "tile", None),
        P(("groups", "dither"), "tile", None),
        P(("groups", "tile", "dither", "band"), None),
        P(("groups", "tile", "dither", "band")),
        P(("groups", "tile", "dither", "band"), None),
        P(("groups", "tile", "dither", "band")),
        P(("groups", "tile", "dither", "band")),
    )
    out_specs = (P(("groups", "tile", "dither"), "band"), P(("groups", "dither"), "tile", None))
    fn = functools.partial(per_device, mesh.shape["tile"], mesh.shape["dither"])
    return jax.shard_map(fn, mesh=mesh, in_specs=in_specs, out_specs=out_specs, check_vma=False)
```

```python
import functools

import jax
import jax.numpy as jnp
from jax import lax
from jax.experimental import pallas as pl
from jax.experimental.pallas import tpu as pltpu
from jax.sharding import PartitionSpec as P

MESH = pl.DeviceIdType.MESH
F32, BF16 = jnp.float32, jnp.bfloat16


def dot(a, b):
    return jnp.dot(a, b, preferred_element_type=F32)


def kernel(
    cfg,
    spectra_ref, psf_ref, obs_ref, bad_ref, tile_ref, slot_ref, src_ref, blk_ref, kind_ref,
    grad_ref, res_ref,
    cols, traces, masked, onehot, onehot_t, psf_f, psf_t, own, fsend, frecv, zrecv, zsend,
    resid, rows, terms, dsend, drecv,
    fs_sem, fr_sem, zs_sem, zr_sem, gs_sem, gr_sem, ps_sem, pr_sem, ds_sem, dr_sem,
):
    n, nd, parts, sub = cfg
    entries = tile_ref.shape[1]
    slots = obs_ref.shape[0]
    half = slots // 2
    kinds, bins, pixels = psf_ref.shape
    sources, wide = spectra_ref.shape
    blocks = wide // bins
    fold = kinds // 2
    step_rows = min(256, entries)
    z = lax.axis_index("tile")
    b = lax.axis_index("band")
    d = lax.axis_index("dither")
    peer = {"band": 1 - b}
    above, below = {"tile": z + 1}, {"tile": z - 1}
    has_above, has_below = z < n - 1, z > 0

    barrier = pltpu.get_barrier_semaphore()

    def greet(where):
        pl.semaphore_signal(barrier, inc=1, device_id=where, device_id_type=MESH)

    greet(peer)
    pl.when(has_above)(lambda: greet(above))
    pl.when(has_below)(lambda: greet(below))
    for k in range(1, nd):
        greet({"dither": lax.rem(d + k, nd)})

    stack = [tile_ref[...], slot_ref[...], src_ref[...], blk_ref[...], kind_ref[...]]
    cols[...] = jnp.concatenate(stack + [kind_ref[...]] * 3, axis=0).T

    def spread(values, which, count):
        return jnp.concatenate(
            [jnp.where(which == k, values, 0.0).astype(BF16) for k in range(count)], axis=1
        )

    def through(values, kind, table):
        low = kind < fold
        product = dot(spread(values, jnp.where(low, kind, kind - fold), fold), table[...])
        width = product.shape[1] // 2
        return jnp.where(low, product[:, :width], product[:, width:])

    flat = psf_ref[...].reshape(kinds * bins, pixels)
    psf_f[:, 0:pixels] = flat[:fold * bins]
    psf_f[:, pixels:2 * pixels] = flat[fold * bins:]

    def forward(i, _):
        at = pl.ds(pl.multiple_of(i * step_rows, step_rows), step_rows)
        col = cols[at, :]
        lane = lax.broadcasted_iota(jnp.int32, (step_rows, sources), 1)
        pick = jnp.where(lane == col[:, 2:3], 1.0, 0.0).astype(BF16)
        found = dot(pick, spectra_ref[...])
        block = jnp.broadcast_to(col[:, 3:4], (step_rows, bins))
        value = jnp.zeros((step_rows, bins), F32)
        for k in range(blocks):
            value = jnp.where(block == k, found[:, k * bins:(k + 1) * bins], value)
        kind = jnp.broadcast_to(col[:, 4:5], (step_rows, bins))
        traces[at, :] = through(value, kind, psf_f).astype(BF16)
        return _

    lax.fori_loop(0, entries // step_rows, forward, 0)

    def mark(i, _):
        size = 128
        at = pl.ds(pl.multiple_of(i * size, size), size)
        row = lax.broadcasted_iota(jnp.int32, (size, entries), 0) + i * size
        onehot[at, :] = jnp.where(row == slot_ref[...], 1.0, 0.0).astype(BF16)
        return _

    lax.fori_loop(0, slots // 128, mark, 0)

    pl.semaphore_wait(barrier, 1 + (nd - 1) + has_above.astype(jnp.int32) + has_below.astype(jnp.int32))

    def my_rows(c):
        return pl.ds(pl.multiple_of(b * half + c * sub, sub), sub)

    def peer_rows(c):
        return pl.ds(pl.multiple_of((1 - b) * half + c * sub, sub), sub)

    def copy(src, dst, send, recv, where):
        return pltpu.make_async_remote_copy(
            src_ref=src, dst_ref=dst, send_sem=send, recv_sem=recv,
            device_id=where, device_id_type=MESH,
        )

    def f_copy(t, c):
        return copy(fsend.at[t, c], frecv.at[t, c], fs_sem.at[t, c], fr_sem.at[t, c], peer)

    def z_copy(way, t, c):
        return copy(
            zsend.at[t, c], zrecv.at[way, t, c], zs_sem.at[t, c], zr_sem.at[way, t, c],
            below if way else above,
        )

    def g_copy(way, t, c):
        block = resid.at[t, my_rows(c)]
        return copy(
            block, block, gs_sem.at[way, t, c], gr_sem.at[way, t, c], below if way else above
        )

    def p_copy(t, c, arriving=False):
        block = resid.at[t, peer_rows(c) if arriving else my_rows(c)]
        return copy(block, block, ps_sem.at[t, c], pr_sem.at[t, c], peer)

    def scatter(t, c):
        tile = jnp.broadcast_to(cols[:, 0:1], (entries, pixels))
        masked[...] = jnp.where(tile == t, traces[...].astype(F32), 0.0).astype(BF16)
        fsend[t, c] = dot(onehot[peer_rows(c), :], masked[...]).astype(BF16)
        f_copy(t, c).start()
        own[t, c] = dot(onehot[my_rows(c), :], masked[...])

    def up_tile(s):
        return n - 1 - s + z

    def down_tile(s):
        return s - (n - 1 - z)

    def both(s, act):
        pl.when(s >= z)(lambda: act(0, up_tile(s)))
        pl.when(s >= n - 1 - z)(lambda: act(1, down_tile(s)))

    def scatter_step(s, c):
        both(s, lambda way, t: scatter(t, c))

    def take(way, t, c):
        def go():
            z_copy(way, t, c).wait_recv()
            own[t, c] = own[t, c] + zrecv[way, t, c].astype(F32)

        pl.when(has_above if way else has_below)(go)

    def reduce_step(s, c):
        def act(way, t):
            f_copy(t, c).wait_recv()
            own[t, c] = own[t, c] + frecv[t, c].astype(F32)
            take(way, t, c)
            zsend[t, c] = own[t, c].astype(BF16)
            z_copy(way, t, c).start()

        both(s, act)

    def pass_on(way, t, c):
        pl.when(has_below if way else has_above)(lambda: g_copy(way, t, c).start())

    def finish(c):
        f_copy(z, c).wait_recv()
        own[z, c] = own[z, c] + frecv[z, c].astype(F32)
        take(0, z, c)
        take(1, z, c)
        at = my_rows(c)
        out = bad_ref[at, :].astype(F32) * (own[z, c] - obs_ref[at, :].astype(F32))
        resid[z, at, :] = out.astype(BF16)
        pass_on(0, z, c)
        pass_on(1, z, c)
        p_copy(z, c).start()

    def around(s, act):
        pl.when(z - s >= 0)(lambda: act(0, z - s))
        pl.when(z + s <= n - 1)(lambda: act(1, z + s))

    def gather_step(s, c):
        def act(way, t):
            g_copy(way, t, c).wait_recv()
            pass_on(way, t, c)
            p_copy(t, c).start()

        around(s, act)

    def use(t, c):
        p_copy(t, c, arriving=True).wait_recv()

        def block(i, _):
            at = pl.ds(pl.multiple_of(i * step_rows, step_rows), step_rows)
            got = dot(onehot_t[at, my_rows(c)], resid[t, my_rows(c), :])
            got = got + dot(onehot_t[at, peer_rows(c)], resid[t, peer_rows(c), :])
            tile = jnp.broadcast_to(cols[at, 0:1], (step_rows, pixels))
            rows[at, :] = rows[at, :] + jnp.where(tile == t, got, 0.0)
            return _

        lax.fori_loop(0, entries // step_rows, block, 0)

    def loop(first, last, act):
        def body(s, _):
            act(s)
            return _

        lax.fori_loop(first, last, body, 0)

    def prepare():
        rows[...] = jnp.zeros_like(rows)

        def turn(k, _):
            at = pl.ds(pl.multiple_of(k * pixels, pixels), pixels)
            psf_t[at, 0:bins] = psf_ref[k].T
            psf_t[at, bins:2 * bins] = psf_ref[k + fold].T
            return _

        lax.fori_loop(0, fold, turn, 0)

        def mark_t(i, _):
            size = 128
            at = pl.ds(pl.multiple_of(i * size, size), size)
            lane = lax.broadcasted_iota(jnp.int32, (size, slots), 1)
            onehot_t[at, :] = jnp.where(lane == cols[at, 1:2], 1.0, 0.0).astype(BF16)
            return _

        lax.fori_loop(0, entries // 128, mark_t, 0)

    middle = has_above & has_below

    def use_around(s, c):
        around(s, lambda way, t: use(t, c))

    def scatter_after(s, c):
        pl.when(s < n - 2)(lambda: scatter_step(s + 1, c))
        pl.when(s == n - 2)(lambda: scatter(z, c))

    for c in range(parts + 1):
        if c < parts:
            scatter_step(0, c)
            scatter_after(0, c)
            reduce_step(0, c)
        if c == 0:
            pl.when(middle)(prepare)
        if c == 1:
            pl.when(jnp.logical_not(middle))(prepare)
        if c >= 2:
            gather_step(n - 1, c - 2)
        if c >= 1:
            finish(c - 1)
        if c >= 2:
            use_around(n - 2, c - 2)
            use_around(n - 1, c - 2)

        def phase(s):
            if c < parts:
                scatter_after(s, c)
                reduce_step(s, c)
            if c >= 1:
                gather_step(s, c - 1)
                pl.when(s == 1)(lambda: use(z, c - 1))
                pl.when(s > 1)(lambda: use_around(s - 1, c - 1))

        loop(1, n - 1, phase)
    gather_step(n - 1, parts - 1)
    use_around(n - 2, parts - 1)
    use_around(n - 1, parts - 1)

    res_ref[...] = resid[z]

    def backward(i, _):
        at = pl.ds(pl.multiple_of(i * step_rows, step_rows), step_rows)
        col = cols[at, :]
        kind = jnp.broadcast_to(col[:, 4:5], (step_rows, pixels))
        term = through(rows[at, :], kind, psf_t)
        block = jnp.broadcast_to(col[:, 3:4], (step_rows, bins))
        terms[at, :] = spread(term, block, blocks)
        return _

    lax.fori_loop(0, entries // step_rows, backward, 0)

    share = sources // nd

    def summed(to):
        row = lax.broadcasted_iota(jnp.int32, (share, entries), 0) + to * share
        member = jnp.where(row == src_ref[...], 1.0, 0.0).astype(BF16)
        return dot(member, terms[...])

    def d_copy(k):
        to = lax.rem(d + k, nd)
        return copy(
            dsend.at[k - 1], drecv.at[k - 1], ds_sem.at[k - 1], dr_sem.at[k - 1], {"dither": to}
        )

    for k in range(1, nd):
        dsend[k - 1] = summed(lax.rem(d + k, nd)).astype(BF16)
        d_copy(k).start()
    grad_ref[...] = summed(d)
    for k in range(1, nd):
        d_copy(k).wait_recv()
        grad_ref[...] = grad_ref[...] + drecv[k - 1].astype(F32)
        d_copy(k).wait_send()

    for c in range(parts):
        loop(0, n, lambda t: f_copy(t, c).wait_send())
        loop(0, n - 1, lambda s: both(s, lambda way, t: z_copy(way, t, c).wait_send()))

        def sent(way, t):
            pl.when(has_below if way else has_above)(lambda: g_copy(way, t, c).wait_send())

        sent(0, z)
        sent(1, z)
        loop(1, n, lambda s: around(s, sent))
        loop(0, n, lambda t: p_copy(t, c).wait_send())


def per_device(
    n, nd, spectra, psf_blocks, observed, bad_mask,
    trace_tile, trace_slot, trace_source, trace_block, psf_index,
):
    entries = trace_slot.shape[0]
    slots, pixels = observed.shape[1:]
    kinds, bins, _ = psf_blocks.shape
    sources, wide = spectra.shape
    parts = 2
    sub = slots // 2 // parts
    row = lambda a: a.reshape(1, entries)
    dma = pltpu.SemaphoreType.DMA
    grad, res = pl.pallas_call(
        functools.partial(kernel, (n, nd, parts, sub)),
        out_shape=(
            jax.ShapeDtypeStruct((sources // nd, wide), F32),
            jax.ShapeDtypeStruct((slots, pixels), BF16),
        ),
        in_specs=[pl.BlockSpec(memory_space=pltpu.VMEM)] * 9,
        out_specs=[pl.BlockSpec(memory_space=pltpu.VMEM)] * 2,
        scratch_shapes=[
            pltpu.VMEM((entries, 8), jnp.int32),
            pltpu.VMEM((entries, pixels), BF16),
            pltpu.VMEM((entries, pixels), BF16),
            pltpu.VMEM((slots, entries), BF16),
            pltpu.VMEM((entries, slots), BF16),
            pltpu.VMEM((kinds // 2 * bins, 2 * pixels), BF16),
            pltpu.VMEM((kinds // 2 * pixels, 2 * bins), BF16),
            pltpu.VMEM((n, parts, sub, pixels), F32),
            pltpu.VMEM((n, parts, sub, pixels), BF16),
            pltpu.VMEM((n, parts, sub, pixels), BF16),
            pltpu.VMEM((2, n, parts, sub, pixels), BF16),
            pltpu.VMEM((n, parts, sub, pixels), BF16),
            pltpu.VMEM((n, slots, pixels), BF16),
            pltpu.VMEM((entries, pixels), F32),
            pltpu.VMEM((entries, wide), BF16),
            pltpu.VMEM((nd - 1, sources // nd, wide), BF16),
            pltpu.VMEM((nd - 1, sources // nd, wide), BF16),
            dma((n, parts)), dma((n, parts)),
            dma((n, parts)), dma((2, n, parts)),
            dma((2, n, parts)), dma((2, n, parts)),
            dma((n, parts)), dma((n, parts)),
            dma((nd - 1,)), dma((nd - 1,)),
        ],
        compiler_params=pltpu.CompilerParams(
            collective_id=0, has_side_effects=True, vmem_limit_bytes=56 * 1024 * 1024
        ),
        cost_estimate=pl.CostEstimate(
            flops=2 * entries * pixels * (2 * kinds * bins + 2 * n * slots + 8 * sources),
            bytes_accessed=2 * 1024 * 1024,
            transcendentals=0,
        ),
    )(
        spectra, psf_blocks, observed[0], bad_mask[0],
        row(trace_tile), row(trace_slot), row(trace_source), row(trace_block), row(psf_index),
    )
    return grad, res[None]


def solution(mesh):
    in_specs = (
        P(("groups", "tile"), "band"),
        P(),
        P(("groups", "dither"), "tile", None),
        P(("groups", "dither"), "tile", None),
        P(("groups", "tile", "dither", "band"), None),
        P(("groups", "tile", "dither", "band")),
        P(("groups", "tile", "dither", "band"), None),
        P(("groups", "tile", "dither", "band")),
        P(("groups", "tile", "dither", "band")),
    )
    out_specs = (P(("groups", "tile", "dither"), "band"), P(("groups", "dither"), "tile", None))
    fn = functools.partial(per_device, mesh.shape["tile"], mesh.shape["dither"])
    return jax.shard_map(fn, mesh=mesh, in_specs=in_specs, out_specs=out_specs, check_vma=False)
```

```python
import functools

import jax
import jax.numpy as jnp
from jax import lax
from jax.experimental import pallas as pl
from jax.experimental.pallas import tpu as pltpu
from jax.sharding import PartitionSpec as P

MESH = pl.DeviceIdType.MESH
F32, BF16 = jnp.float32, jnp.bfloat16


def dot(a, b):
    return jnp.dot(a, b, preferred_element_type=F32)


def kernel(
    cfg,
    spectra_ref, psf_ref, obs_ref, bad_ref, tile_ref, slot_ref, src_ref, blk_ref, kind_ref,
    grad_ref, res_ref,
    cols, traces, masked, onehot, onehot_t, psf_f, psf_t, own, fsend, frecv, zrecv, zsend,
    resid, rows, terms, dsend, drecv,
    fs_sem, fr_sem, zs_sem, zr_sem, gs_sem, gr_sem, ps_sem, pr_sem, ds_sem, dr_sem,
):
    n, nd, parts, sub = cfg
    entries = tile_ref.shape[1]
    slots = obs_ref.shape[0]
    half = slots // 2
    kinds, bins, pixels = psf_ref.shape
    sources, wide = spectra_ref.shape
    blocks = wide // bins
    fold = kinds // 2
    step_rows = min(256, entries)
    z = lax.axis_index("tile")
    b = lax.axis_index("band")
    d = lax.axis_index("dither")
    peer = {"band": 1 - b}
    above, below = {"tile": z + 1}, {"tile": z - 1}
    has_above, has_below = z < n - 1, z > 0

    barrier = pltpu.get_barrier_semaphore()

    def greet(where):
        pl.semaphore_signal(barrier, inc=1, device_id=where, device_id_type=MESH)

    greet(peer)
    pl.when(has_above)(lambda: greet(above))
    pl.when(has_below)(lambda: greet(below))
    for k in range(1, nd):
        greet({"dither": lax.rem(d + k, nd)})

    stack = [tile_ref[...], slot_ref[...], src_ref[...], blk_ref[...], kind_ref[...]]
    cols[...] = jnp.concatenate(stack + [kind_ref[...]] * 3, axis=0).T

    def spread(values, which, count):
        return jnp.concatenate(
            [jnp.where(which == k, values, 0.0).astype(BF16) for k in range(count)], axis=1
        )

    def through(values, kind, table):
        low = kind < fold
        product = dot(spread(values, jnp.where(low, kind, kind - fold), fold), table[...])
        width = product.shape[1] // 2
        return jnp.where(low, product[:, :width], product[:, width:])

    flat = psf_ref[...].reshape(kinds * bins, pixels)
    psf_f[:, 0:pixels] = flat[:fold * bins]
    psf_f[:, pixels:2 * pixels] = flat[fold * bins:]

    def forward(i, _):
        at = pl.ds(pl.multiple_of(i * step_rows, step_rows), step_rows)
        col = cols[at, :]
        lane = lax.broadcasted_iota(jnp.int32, (step_rows, sources), 1)
        pick = jnp.where(lane == col[:, 2:3], 1.0, 0.0).astype(BF16)
        found = dot(pick, spectra_ref[...])
        block = jnp.broadcast_to(col[:, 3:4], (step_rows, bins))
        value = jnp.zeros((step_rows, bins), F32)
        for k in range(blocks):
            value = jnp.where(block == k, found[:, k * bins:(k + 1) * bins], value)
        kind = jnp.broadcast_to(col[:, 4:5], (step_rows, bins))
        traces[at, :] = through(value, kind, psf_f).astype(BF16)
        return _

    lax.fori_loop(0, entries // step_rows, forward, 0)

    def mark(i, _):
        size = 128
        at = pl.ds(pl.multiple_of(i * size, size), size)
        row = lax.broadcasted_iota(jnp.int32, (size, entries), 0) + i * size
        onehot[at, :] = jnp.where(row == slot_ref[...], 1.0, 0.0).astype(BF16)
        return _

    lax.fori_loop(0, slots // 128, mark, 0)

    pl.semaphore_wait(barrier, 1 + (nd - 1) + has_above.astype(jnp.int32) + has_below.astype(jnp.int32))

    def my_rows(c):
        return pl.ds(pl.multiple_of(b * half + c * sub, sub), sub)

    def peer_rows(c):
        return pl.ds(pl.multiple_of((1 - b) * half + c * sub, sub), sub)

    def copy(src, dst, send, recv, where):
        return pltpu.make_async_remote_copy(
            src_ref=src, dst_ref=dst, send_sem=send, recv_sem=recv,
            device_id=where, device_id_type=MESH,
        )

    def f_copy(t, c):
        return copy(fsend.at[t, c], frecv.at[t, c], fs_sem.at[t, c], fr_sem.at[t, c], peer)

    def z_copy(way, t, c):
        return copy(
            zsend.at[t, c], zrecv.at[way, t, c], zs_sem.at[t, c], zr_sem.at[way, t, c],
            below if way else above,
        )

    def g_copy(way, t, c):
        block = resid.at[t, my_rows(c)]
        return copy(
            block, block, gs_sem.at[way, t, c], gr_sem.at[way, t, c], below if way else above
        )

    def p_copy(t, c, arriving=False):
        block = resid.at[t, peer_rows(c) if arriving else my_rows(c)]
        return copy(block, block, ps_sem.at[t, c], pr_sem.at[t, c], peer)

    def scatter(t, c):
        tile = jnp.broadcast_to(cols[:, 0:1], (entries, pixels))
        masked[...] = jnp.where(tile == t, traces[...].astype(F32), 0.0).astype(BF16)
        fsend[t, c] = dot(onehot[peer_rows(c), :], masked[...]).astype(BF16)
        f_copy(t, c).start()
        own[t, c] = dot(onehot[my_rows(c), :], masked[...])

    def up_tile(s):
        return n - 1 - s + z

    def down_tile(s):
        return s - (n - 1 - z)

    def both(s, act):
        pl.when(s >= z)(lambda: act(0, up_tile(s)))
        pl.when(s >= n - 1 - z)(lambda: act(1, down_tile(s)))

    def scatter_step(s, c):
        both(s, lambda way, t: scatter(t, c))

    def take(way, t, c):
        def go():
            z_copy(way, t, c).wait_recv()
            own[t, c] = own[t, c] + zrecv[way, t, c].astype(F32)

        pl.when(has_above if way else has_below)(go)

    def reduce_step(s, c):
        def act(way, t):
            f_copy(t, c).wait_recv()
            own[t, c] = own[t, c] + frecv[t, c].astype(F32)
            take(way, t, c)
            zsend[t, c] = own[t, c].astype(BF16)
            z_copy(way, t, c).start()

        both(s, act)

    def pass_on(way, t, c):
        pl.when(has_below if way else has_above)(lambda: g_copy(way, t, c).start())

    def finish(c):
        f_copy(z, c).wait_recv()
        own[z, c] = own[z, c] + frecv[z, c].astype(F32)
        take(0, z, c)
        take(1, z, c)
        at = my_rows(c)
        out = bad_ref[at, :].astype(F32) * (own[z, c] - obs_ref[at, :].astype(F32))
        resid[z, at, :] = out.astype(BF16)
        pass_on(0, z, c)
        pass_on(1, z, c)
        p_copy(z, c).start()

    def around(s, act):
        pl.when(z - s >= 0)(lambda: act(0, z - s))
        pl.when(z + s <= n - 1)(lambda: act(1, z + s))

    def gather_step(s, c):
        def act(way, t):
            g_copy(way, t, c).wait_recv()
            pass_on(way, t, c)
            p_copy(t, c).start()

        around(s, act)

    def use(t, c):
        p_copy(t, c, arriving=True).wait_recv()

        def block(i, _):
            at = pl.ds(pl.multiple_of(i * step_rows, step_rows), step_rows)
            got = dot(onehot_t[at, my_rows(c)], resid[t, my_rows(c), :])
            got = got + dot(onehot_t[at, peer_rows(c)], resid[t, peer_rows(c), :])
            tile = jnp.broadcast_to(cols[at, 0:1], (step_rows, pixels))
            rows[at, :] = rows[at, :] + jnp.where(tile == t, got, 0.0)
            return _

        lax.fori_loop(0, entries // step_rows, block, 0)

    def loop(first, last, act):
        def body(s, _):
            act(s)
            return _

        lax.fori_loop(first, last, body, 0)

    def prepare():
        rows[...] = jnp.zeros_like(rows)

        def turn(k, _):
            at = pl.ds(pl.multiple_of(k * pixels, pixels), pixels)
            psf_t[at, 0:bins] = psf_ref[k].T
            psf_t[at, bins:2 * bins] = psf_ref[k + fold].T
            return _

        lax.fori_loop(0, fold, turn, 0)

        def mark_t(i, _):
            size = 128
            at = pl.ds(pl.multiple_of(i * size, size), size)
            lane = lax.broadcasted_iota(jnp.int32, (size, slots), 1)
            onehot_t[at, :] = jnp.where(lane == cols[at, 1:2], 1.0, 0.0).astype(BF16)
            return _

        lax.fori_loop(0, entries // 128, mark_t, 0)

    middle = has_above & has_below

    def use_around(s, c):
        around(s, lambda way, t: use(t, c))

    def scatter_after(s, c):
        pl.when(s < n - 2)(lambda: scatter_step(s + 1, c))
        pl.when(s == n - 2)(lambda: scatter(z, c))

    for c in range(parts + 1):
        if c < parts:
            scatter_step(0, c)
            scatter_after(0, c)
            reduce_step(0, c)
        if c == 0:
            pl.when(middle)(prepare)
        if c == 1:
            pl.when(jnp.logical_not(middle))(prepare)
        if c >= 2:
            gather_step(n - 1, c - 2)
        if c >= 1:
            finish(c - 1)
        if c >= 2:
            use_around(n - 2, c - 2)
            use_around(n - 1, c - 2)

        def phase(s):
            if c < parts:
                scatter_after(s, c)
                reduce_step(s, c)
            if c >= 1:
                gather_step(s, c - 1)
                pl.when(s == 1)(lambda: use(z, c - 1))
                pl.when(s > 1)(lambda: use_around(s - 1, c - 1))

        loop(1, n - 1, phase)
    gather_step(n - 1, parts - 1)
    use_around(n - 2, parts - 1)
    use_around(n - 1, parts - 1)

    res_ref[...] = resid[z]

    def backward(i, _):
        at = pl.ds(pl.multiple_of(i * step_rows, step_rows), step_rows)
        col = cols[at, :]
        kind = jnp.broadcast_to(col[:, 4:5], (step_rows, pixels))
        term = through(rows[at, :], kind, psf_t)
        block = jnp.broadcast_to(col[:, 3:4], (step_rows, bins))
        terms[at, :] = spread(term, block, blocks)
        return _

    lax.fori_loop(0, entries // step_rows, backward, 0)

    share = sources // nd

    def summed(to):
        row = lax.broadcasted_iota(jnp.int32, (share, entries), 0) + to * share
        member = jnp.where(row == src_ref[...], 1.0, 0.0).astype(BF16)
        return dot(member, terms[...])

    def d_copy(k):
        to = lax.rem(d + k, nd)
        return copy(
            dsend.at[k - 1], drecv.at[k - 1], ds_sem.at[k - 1], dr_sem.at[k - 1], {"dither": to}
        )

    for k in range(1, nd):
        dsend[k - 1] = summed(lax.rem(d + k, nd)).astype(BF16)
        d_copy(k).start()
    grad_ref[...] = summed(d)
    for k in range(1, nd):
        d_copy(k).wait_recv()
        grad_ref[...] = grad_ref[...] + drecv[k - 1].astype(F32)
        d_copy(k).wait_send()

    for c in range(parts):
        loop(0, n, lambda t: f_copy(t, c).wait_send())
        loop(0, n - 1, lambda s: both(s, lambda way, t: z_copy(way, t, c).wait_send()))

        def sent(way, t):
            pl.when(has_below if way else has_above)(lambda: g_copy(way, t, c).wait_send())

        sent(0, z)
        sent(1, z)
        loop(1, n, lambda s: around(s, sent))
        loop(0, n, lambda t: p_copy(t, c).wait_send())


def per_device(
    n, nd, spectra, psf_blocks, observed, bad_mask,
    trace_tile, trace_slot, trace_source, trace_block, psf_index,
):
    entries = trace_slot.shape[0]
    slots, pixels = observed.shape[1:]
    kinds, bins, _ = psf_blocks.shape
    sources, wide = spectra.shape
    parts = 1
    sub = slots // 2 // parts
    row = lambda a: a.reshape(1, entries)
    dma = pltpu.SemaphoreType.DMA
    grad, res = pl.pallas_call(
        functools.partial(kernel, (n, nd, parts, sub)),
        out_shape=(
            jax.ShapeDtypeStruct((sources // nd, wide), F32),
            jax.ShapeDtypeStruct((slots, pixels), BF16),
        ),
        in_specs=[pl.BlockSpec(memory_space=pltpu.VMEM)] * 9,
        out_specs=[pl.BlockSpec(memory_space=pltpu.VMEM)] * 2,
        scratch_shapes=[
            pltpu.VMEM((entries, 8), jnp.int32),
            pltpu.VMEM((entries, pixels), BF16),
            pltpu.VMEM((entries, pixels), BF16),
            pltpu.VMEM((slots, entries), BF16),
            pltpu.VMEM((entries, slots), BF16),
            pltpu.VMEM((kinds // 2 * bins, 2 * pixels), BF16),
            pltpu.VMEM((kinds // 2 * pixels, 2 * bins), BF16),
            pltpu.VMEM((n, parts, sub, pixels), F32),
            pltpu.VMEM((n, parts, sub, pixels), BF16),
            pltpu.VMEM((n, parts, sub, pixels), BF16),
            pltpu.VMEM((2, n, parts, sub, pixels), BF16),
            pltpu.VMEM((n, parts, sub, pixels), BF16),
            pltpu.VMEM((n, slots, pixels), BF16),
            pltpu.VMEM((entries, pixels), F32),
            pltpu.VMEM((entries, wide), BF16),
            pltpu.VMEM((nd - 1, sources // nd, wide), BF16),
            pltpu.VMEM((nd - 1, sources // nd, wide), BF16),
            dma((n, parts)), dma((n, parts)),
            dma((n, parts)), dma((2, n, parts)),
            dma((2, n, parts)), dma((2, n, parts)),
            dma((n, parts)), dma((n, parts)),
            dma((nd - 1,)), dma((nd - 1,)),
        ],
        compiler_params=pltpu.CompilerParams(
            collective_id=0, has_side_effects=True, vmem_limit_bytes=56 * 1024 * 1024
        ),
        cost_estimate=pl.CostEstimate(
            flops=2 * entries * pixels * (2 * kinds * bins + 2 * n * slots + 8 * sources),
            bytes_accessed=2 * 1024 * 1024,
            transcendentals=0,
        ),
    )(
        spectra, psf_blocks, observed[0], bad_mask[0],
        row(trace_tile), row(trace_slot), row(trace_source), row(trace_block), row(psf_index),
    )
    return grad, res[None]


def solution(mesh):
    in_specs = (
        P(("groups", "tile"), "band"),
        P(),
        P(("groups", "dither"), "tile", None),
        P(("groups", "dither"), "tile", None),
        P(("groups", "tile", "dither", "band"), None),
        P(("groups", "tile", "dither", "band")),
        P(("groups", "tile", "dither", "band"), None),
        P(("groups", "tile", "dither", "band")),
        P(("groups", "tile", "dither", "band")),
    )
    out_specs = (P(("groups", "tile", "dither"), "band"), P(("groups", "dither"), "tile", None))
    fn = functools.partial(per_device, mesh.shape["tile"], mesh.shape["dither"])
    return jax.shard_map(fn, mesh=mesh, in_specs=in_specs, out_specs=out_specs, check_vma=False)
```

```python
import functools

import jax
import jax.numpy as jnp
from jax import lax
from jax.experimental import pallas as pl
from jax.experimental.pallas import tpu as pltpu
from jax.sharding import PartitionSpec as P

MESH = pl.DeviceIdType.MESH
F32, BF16 = jnp.float32, jnp.bfloat16


def dot(a, b):
    return jnp.dot(a, b, preferred_element_type=F32)


def kernel(
    cfg,
    spectra_ref, psf_ref, obs_ref, bad_ref, tile_ref, slot_ref, src_ref, blk_ref, kind_ref,
    grad_ref, res_ref,
    cols, traces, masked, onehot, onehot_t, psf_f, psf_t, own, fsend, frecv, zrecv, zsend,
    resid, rows, terms, dsend, drecv,
    fs_sem, fr_sem, zs_sem, zr_sem, gs_sem, gr_sem, ps_sem, pr_sem, ds_sem, dr_sem,
):
    n, nd, steps = cfg
    entries = tile_ref.shape[1]
    slots = obs_ref.shape[0]
    half = slots // 2
    kinds, bins, pixels = psf_ref.shape
    sources, wide = spectra_ref.shape
    blocks = wide // bins
    fold = kinds // 2
    step_rows = min(256, entries, half)
    z = lax.axis_index("tile")
    b = lax.axis_index("band")
    d = lax.axis_index("dither")
    peer = {"band": 1 - b}

    def bit(k):
        return lax.rem(z // (1 << k), 2)

    def partner(k):
        return {"tile": z + (1 - 2 * bit(k)) * (1 << k)}

    def kept(k, h):
        return h * (2 << k) + lax.rem(z, 2 << k)

    def other(k, h):
        return h * (2 << k) + (1 - bit(k)) * (1 << k) + lax.rem(z, 1 << k)

    barrier = pltpu.get_barrier_semaphore()

    def greet(where):
        pl.semaphore_signal(barrier, inc=1, device_id=where, device_id_type=MESH)

    greet(peer)
    for k in range(steps):
        greet(partner(k))
    for k in range(1, nd):
        greet({"dither": lax.rem(d + k, nd)})

    def loop(count, act, unroll=False):
        def body(s, _):
            act(s)
            return _

        lax.fori_loop(0, count, body, 0, unroll=unroll)

    def span(i, size, base=0):
        return pl.ds(pl.multiple_of(base + i * size, size), size)

    stack = [tile_ref[...], slot_ref[...], src_ref[...], blk_ref[...], kind_ref[...]]
    cols[...] = jnp.concatenate(stack + [kind_ref[...]] * 3, axis=0).T

    def spread(values, which, count):
        return jnp.concatenate(
            [jnp.where(which == k, values, 0.0).astype(BF16) for k in range(count)], axis=1
        )

    def through(values, kind, table):
        low = kind < fold
        product = dot(spread(values, jnp.where(low, kind, kind - fold), fold), table[...])
        width = product.shape[1] // 2
        return jnp.where(low, product[:, :width], product[:, width:])

    flat = psf_ref[...].reshape(kinds * bins, pixels)
    psf_f[:, 0:pixels] = flat[:fold * bins]
    psf_f[:, pixels:2 * pixels] = flat[fold * bins:]

    def forward(i):
        at = span(i, step_rows)
        col = cols[at, :]
        lane = lax.broadcasted_iota(jnp.int32, (step_rows, sources), 1)
        pick = jnp.where(lane == col[:, 2:3], 1.0, 0.0).astype(BF16)
        found = dot(pick, spectra_ref[...])
        block = jnp.broadcast_to(col[:, 3:4], (step_rows, bins))
        value = jnp.zeros((step_rows, bins), F32)
        for k in range(blocks):
            value = jnp.where(block == k, found[:, k * bins:(k + 1) * bins], value)
        kind = jnp.broadcast_to(col[:, 4:5], (step_rows, bins))
        traces[at, :] = through(value, kind, psf_f).astype(BF16)

    loop(entries // step_rows, forward, unroll=True)

    def mark(i):
        size = 128
        row = lax.broadcasted_iota(jnp.int32, (size, entries), 0) + i * size
        onehot[span(i, size), :] = jnp.where(row == slot_ref[...], 1.0, 0.0).astype(BF16)

    loop(slots // 128, mark)

    pl.semaphore_wait(barrier, 1 + steps + nd - 1)

    mine, theirs = span(b, half), span(1 - b, half)

    def copy(src, dst, send, recv, where):
        return pltpu.make_async_remote_copy(
            src_ref=src, dst_ref=dst, send_sem=send, recv_sem=recv,
            device_id=where, device_id_type=MESH,
        )

    def f_copy(t):
        return copy(fsend.at[t], frecv.at[t], fs_sem.at[t], fr_sem.at[t], peer)

    def z_copy(k, h):
        t = other(k, h)
        return copy(zsend.at[t], zrecv.at[k, h], zs_sem.at[t], zr_sem.at[k, h], partner(k))

    def g_copy(k, h):
        block = resid.at[kept(k, h), mine]
        return copy(block, block, gs_sem.at[k, h], gr_sem.at[k, h], partner(k))

    def p_copy(t, arriving=False):
        block = resid.at[t, theirs if arriving else mine]
        return copy(block, block, ps_sem.at[t], pr_sem.at[t], peer)

    def scatter(t, u):
        tile = jnp.broadcast_to(cols[:, 0:1], (entries, pixels))
        trace = traces[...].astype(F32)
        masked[:, 0:pixels] = jnp.where(tile == t, trace, 0.0).astype(BF16)
        masked[:, pixels:2 * pixels] = jnp.where(tile == u, trace, 0.0).astype(BF16)

        def away(i):
            part = dot(onehot[span(i, step_rows, (1 - b) * half), :], masked[...]).astype(BF16)
            fsend[t, span(i, step_rows), :] = part[:, 0:pixels]
            fsend[u, span(i, step_rows), :] = part[:, pixels:2 * pixels]

        loop(half // step_rows, away, unroll=True)
        f_copy(t).start()
        f_copy(u).start()

        def here(i):
            part = dot(onehot[span(i, step_rows, b * half), :], masked[...])
            own[t, span(i, step_rows), :] = part[:, 0:pixels]
            own[u, span(i, step_rows), :] = part[:, pixels:2 * pixels]

        loop(half // step_rows, here, unroll=True)

    def total(t, k):
        f_copy(t).wait_recv()
        value = own[t] + frecv[t].astype(F32)
        for j in range(k):
            z_copy(j, t // (2 << j)).wait_recv()
            value = value + zrecv[j, t // (2 << j)].astype(F32)
        return value

    loop(n // 4, lambda j: scatter(other(0, 2 * j), other(0, 2 * j + 1)))
    loop(n // 4, lambda j: scatter(kept(0, 2 * j), kept(0, 2 * j + 1)))

    def reduce_step(k):
        count = n >> (k + 1)

        def send(i):
            h = lax.rem(z // (2 << k) + i + count // 2, count)
            t = other(k, h)
            zsend[t] = total(t, k).astype(BF16)
            z_copy(k, h).start()

        loop(count, send)

    reduce_step(0)

    rows[...] = jnp.zeros_like(rows)

    def turn(k):
        psf_t[span(k, pixels), 0:bins] = psf_ref[k].T
        psf_t[span(k, pixels), bins:2 * bins] = psf_ref[k + fold].T

    loop(fold, turn)

    def mark_t(i):
        size = 128
        lane = lax.broadcasted_iota(jnp.int32, (size, slots), 1)
        slot = cols[span(i, size), 1:2]
        onehot_t[span(i, size), :] = jnp.where(lane == slot, 1.0, 0.0).astype(BF16)

    loop(entries // 128, mark_t)

    for k in range(1, steps):
        reduce_step(k)
    model = total(z, steps)
    out = bad_ref[mine, :].astype(F32) * (model - obs_ref[mine, :].astype(F32))
    resid[z, mine, :] = out.astype(BF16)

    def pass_on(t, k):
        for j in reversed(range(k)):
            g_copy(j, t // (2 << j)).start()
        p_copy(t).start()

    pass_on(z, steps)

    def use(h):
        def gathered(where):
            pair = jnp.concatenate([resid[2 * h, where, :], resid[2 * h + 1, where, :]], axis=1)

            def block(i):
                at = span(i, step_rows)
                got = dot(onehot_t[at, where], pair)
                tile = jnp.broadcast_to(cols[at, 0:1], (step_rows, pixels))
                value = jnp.where(tile == 2 * h, got[:, 0:pixels], 0.0)
                value = jnp.where(tile == 2 * h + 1, got[:, pixels:2 * pixels], value)
                rows[at, :] = rows[at, :] + value

            loop(entries // step_rows, block, unroll=True)

        gathered(mine)
        p_copy(2 * h, arriving=True).wait_recv()
        p_copy(2 * h + 1, arriving=True).wait_recv()
        gathered(theirs)

    for k in reversed(range(steps)):
        count = n >> (k + 1)

        def arrive(i):
            h = lax.rem(z // (2 << k) + i, count)
            g_copy(k, h).wait_recv()
            pass_on(other(k, h), k)
            if k == 0:
                use(h)

        loop(count, arrive)

    res_ref[...] = resid[z]

    def backward(i):
        at = span(i, step_rows)
        col = cols[at, :]
        kind = jnp.broadcast_to(col[:, 4:5], (step_rows, pixels))
        term = through(rows[at, :], kind, psf_t)
        block = jnp.broadcast_to(col[:, 3:4], (step_rows, bins))
        terms[at, :] = spread(term, block, blocks)

    loop(entries // step_rows, backward, unroll=True)

    share = sources // nd

    def summed(to):
        row = lax.broadcasted_iota(jnp.int32, (share, entries), 0) + to * share
        member = jnp.where(row == src_ref[...], 1.0, 0.0).astype(BF16)
        return dot(member, terms[...])

    def d_copy(k):
        to = lax.rem(d + k, nd)
        return copy(
            dsend.at[k - 1], drecv.at[k - 1], ds_sem.at[k - 1], dr_sem.at[k - 1], {"dither": to}
        )

    for k in range(1, nd):
        dsend[k - 1] = summed(lax.rem(d + k, nd)).astype(BF16)
        d_copy(k).start()
    grad_ref[...] = summed(d)
    for k in range(1, nd):
        d_copy(k).wait_recv()
        grad_ref[...] = grad_ref[...] + drecv[k - 1].astype(F32)
        d_copy(k).wait_send()

    loop(n, lambda t: f_copy(t).wait_send())
    loop(n, lambda t: p_copy(t).wait_send())
    for k in range(steps):
        loop(n >> (k + 1), lambda h: z_copy(k, h).wait_send())
        loop(n >> (k + 1), lambda h: g_copy(k, h).wait_send())


def per_device(
    n, nd, spectra, psf_blocks, observed, bad_mask,
    trace_tile, trace_slot, trace_source, trace_block, psf_index,
):
    entries = trace_slot.shape[0]
    slots, pixels = observed.shape[1:]
    kinds, bins, _ = psf_blocks.shape
    sources, wide = spectra.shape
    half = slots // 2
    steps = n.bit_length() - 1
    row = lambda a: a.reshape(1, entries)
    dma = pltpu.SemaphoreType.DMA
    grad, res = pl.pallas_call(
        functools.partial(kernel, (n, nd, steps)),
        out_shape=(
            jax.ShapeDtypeStruct((sources // nd, wide), F32),
            jax.ShapeDtypeStruct((slots, pixels), BF16),
        ),
        in_specs=[pl.BlockSpec(memory_space=pltpu.VMEM)] * 9,
        out_specs=[pl.BlockSpec(memory_space=pltpu.VMEM)] * 2,
        scratch_shapes=[
            pltpu.VMEM((entries, 8), jnp.int32),
            pltpu.VMEM((entries, pixels), BF16),
            pltpu.VMEM((entries, 2 * pixels), BF16),
            pltpu.VMEM((slots, entries), BF16),
            pltpu.VMEM((entries, slots), BF16),
            pltpu.VMEM((kinds // 2 * bins, 2 * pixels), BF16),
            pltpu.VMEM((kinds // 2 * pixels, 2 * bins), BF16),
            pltpu.VMEM((n, half, pixels), F32),
            pltpu.VMEM((n, half, pixels), BF16),
            pltpu.VMEM((n, half, pixels), BF16),
            pltpu.VMEM((steps, n // 2, half, pixels), BF16),
            pltpu.VMEM((n, half, pixels), BF16),
            pltpu.VMEM((n, slots, pixels), BF16),
            pltpu.VMEM((entries, pixels), F32),
            pltpu.VMEM((entries, wide), BF16),
            pltpu.VMEM((nd - 1, sources // nd, wide), BF16),
            pltpu.VMEM((nd - 1, sources // nd, wide), BF16),
            dma((n,)), dma((n,)),
            dma((n,)), dma((steps, n // 2)),
            dma((steps, n // 2)), dma((steps, n // 2)),
            dma((n,)), dma((n,)),
            dma((nd - 1,)), dma((nd - 1,)),
        ],
        compiler_params=pltpu.CompilerParams(
            collective_id=0, has_side_effects=True, vmem_limit_bytes=56 * 1024 * 1024
        ),
        cost_estimate=pl.CostEstimate(
            flops=2 * entries * pixels * (2 * kinds * bins + 2 * n * slots + 8 * sources),
            bytes_accessed=2 * 1024 * 1024,
            transcendentals=0,
        ),
    )(
        spectra, psf_blocks, observed[0], bad_mask[0],
        row(trace_tile), row(trace_slot), row(trace_source), row(trace_block), row(psf_index),
    )
    return grad, res[None]


def solution(mesh):
    in_specs = (
        P(("groups", "tile"), "band"),
        P(),
        P(("groups", "dither"), "tile", None),
        P(("groups", "dither"), "tile", None),
        P(("groups", "tile", "dither", "band"), None),
        P(("groups", "tile", "dither", "band")),
        P(("groups", "tile", "dither", "band"), None),
        P(("groups", "tile", "dither", "band")),
        P(("groups", "tile", "dither", "band")),
    )
    out_specs = (P(("groups", "tile", "dither"), "band"), P(("groups", "dither"), "tile", None))
    fn = functools.partial(per_device, mesh.shape["tile"], mesh.shape["dither"])
    return jax.shard_map(fn, mesh=mesh, in_specs=in_specs, out_specs=out_specs, check_vma=False)
```

```python
import functools

import jax
import jax.numpy as jnp
from jax import lax
from jax.experimental import pallas as pl
from jax.experimental.pallas import tpu as pltpu
from jax.sharding import PartitionSpec as P

MESH = pl.DeviceIdType.MESH
F32, BF16 = jnp.float32, jnp.bfloat16


def dot(a, b):
    return jnp.dot(a, b, preferred_element_type=F32)


def kernel(
    cfg,
    spectra_ref, psf_ref, obs_ref, bad_ref, tile_ref, slot_ref, src_ref, blk_ref, kind_ref,
    grad_ref, res_ref,
    cols, traces, masked, onehot, onehot_t, psf_f, psf_t, own, fsend, frecv, zrecv, zsend,
    resid, rows, terms, dsend, drecv, obs, bad,
    fs_sem, fr_sem, zs_sem, zr_sem, gs_sem, gr_sem, ps_sem, pr_sem, ds_sem, dr_sem, in_sem,
):
    n, nd, steps, parts = cfg
    entries = tile_ref.shape[1]
    slots = obs_ref.shape[0]
    half = slots // 2
    sub = half // parts
    kinds, bins, pixels = psf_ref.shape
    sources, wide = spectra_ref.shape
    blocks = wide // bins
    fold = kinds // 2
    step_rows = min(256, entries, sub)
    z = lax.axis_index("tile")
    b = lax.axis_index("band")
    d = lax.axis_index("dither")
    peer = {"band": 1 - b}

    def bit(k):
        return lax.rem(z // (1 << k), 2)

    def partner(k):
        return {"tile": z + (1 - 2 * bit(k)) * (1 << k)}

    def kept(k, h):
        return h * (2 << k) + lax.rem(z, 2 << k)

    def other(k, h):
        return h * (2 << k) + (1 - bit(k)) * (1 << k) + lax.rem(z, 1 << k)

    barrier = pltpu.get_barrier_semaphore()

    def greet(where):
        pl.semaphore_signal(barrier, inc=1, device_id=where, device_id_type=MESH)

    greet(peer)
    for k in range(steps):
        greet(partner(k))
    for k in range(1, nd):
        greet({"dither": lax.rem(d + k, nd)})

    def loop(count, act, unroll=False):
        def body(s, _):
            act(s)
            return _

        lax.fori_loop(0, count, body, 0, unroll=unroll)

    def span(i, size, base=0):
        return pl.ds(pl.multiple_of(base + i * size, size), size)

    mine, theirs = span(b, half), span(1 - b, half)
    loads = [
        pltpu.make_async_copy(obs_ref.at[mine], obs, in_sem.at[0]),
        pltpu.make_async_copy(bad_ref.at[mine], bad, in_sem.at[1]),
    ]
    for load in loads:
        load.start()

    stack = [tile_ref[...], slot_ref[...], src_ref[...], blk_ref[...], kind_ref[...]]
    cols[...] = jnp.concatenate(stack + [kind_ref[...]] * 3, axis=0).T

    def spread(values, which, count):
        return jnp.concatenate(
            [jnp.where(which == k, values, 0.0).astype(BF16) for k in range(count)], axis=1
        )

    def through(values, kind, table):
        low = kind < fold
        product = dot(spread(values, jnp.where(low, kind, kind - fold), fold), table[...])
        width = product.shape[1] // 2
        return jnp.where(low, product[:, :width], product[:, width:])

    flat = psf_ref[...].reshape(kinds * bins, pixels)
    psf_f[:, 0:pixels] = flat[:fold * bins]
    psf_f[:, pixels:2 * pixels] = flat[fold * bins:]

    def forward(i):
        at = span(i, step_rows)
        col = cols[at, :]
        lane = lax.broadcasted_iota(jnp.int32, (step_rows, sources), 1)
        pick = jnp.where(lane == col[:, 2:3], 1.0, 0.0).astype(BF16)
        found = dot(pick, spectra_ref[...])
        block = jnp.broadcast_to(col[:, 3:4], (step_rows, bins))
        value = jnp.zeros((step_rows, bins), F32)
        for k in range(blocks):
            value = jnp.where(block == k, found[:, k * bins:(k + 1) * bins], value)
        kind = jnp.broadcast_to(col[:, 4:5], (step_rows, bins))
        traces[at, :] = through(value, kind, psf_f).astype(BF16)

    loop(entries // step_rows, forward, unroll=True)

    def mark(i):
        size = 128
        row = lax.broadcasted_iota(jnp.int32, (size, entries), 0) + i * size
        onehot[span(i, size), :] = jnp.where(row == slot_ref[...], 1.0, 0.0).astype(BF16)

    loop(slots // 128, mark, unroll=True)

    pl.semaphore_wait(barrier, 1 + steps + nd - 1)

    def my_rows(c):
        return span(c, sub, b * half)

    def peer_rows(c):
        return span(c, sub, (1 - b) * half)

    def copy(src, dst, send, recv, where):
        return pltpu.make_async_remote_copy(
            src_ref=src, dst_ref=dst, send_sem=send, recv_sem=recv,
            device_id=where, device_id_type=MESH,
        )

    def f_copy(t, c):
        return copy(fsend.at[t, c], frecv.at[t, c], fs_sem.at[t, c], fr_sem.at[t, c], peer)

    def z_copy(k, h, c):
        t = other(k, h)
        return copy(
            zsend.at[t, c], zrecv.at[k, h, c], zs_sem.at[t, c], zr_sem.at[k, h, c], partner(k)
        )

    def g_copy(k, h, c):
        block = resid.at[kept(k, h), my_rows(c)]
        return copy(block, block, gs_sem.at[k, h, c], gr_sem.at[k, h, c], partner(k))

    def p_copy(t, c, arriving=False):
        block = resid.at[t, peer_rows(c) if arriving else my_rows(c)]
        return copy(block, block, ps_sem.at[t, c], pr_sem.at[t, c], peer)

    def scatter(t, u):
        tile = jnp.broadcast_to(cols[:, 0:1], (entries, pixels))
        trace = traces[...].astype(F32)
        masked[:, 0:pixels] = jnp.where(tile == t, trace, 0.0).astype(BF16)
        masked[:, pixels:2 * pixels] = jnp.where(tile == u, trace, 0.0).astype(BF16)

        for c in range(parts):
            def away(i):
                at = span(i, step_rows, (1 - b) * half + c * sub)
                part = dot(onehot[at, :], masked[...]).astype(BF16)
                fsend[t, c, span(i, step_rows), :] = part[:, 0:pixels]
                fsend[u, c, span(i, step_rows), :] = part[:, pixels:2 * pixels]

            loop(sub // step_rows, away, unroll=True)
            f_copy(t, c).start()
            f_copy(u, c).start()
        for c in range(parts):
            def here(i):
                part = dot(onehot[span(i, step_rows, b * half + c * sub), :], masked[...])
                own[t, c, span(i, step_rows), :] = part[:, 0:pixels]
                own[u, c, span(i, step_rows), :] = part[:, pixels:2 * pixels]

            loop(sub // step_rows, here, unroll=True)

    def total(t, k, c):
        f_copy(t, c).wait_recv()
        value = own[t, c] + frecv[t, c].astype(F32)
        for j in range(k):
            z_copy(j, t // (2 << j), c).wait_recv()
            value = value + zrecv[j, t // (2 << j), c].astype(F32)
        return value

    loop(n // 4, lambda j: scatter(other(0, 2 * j), other(0, 2 * j + 1)))
    loop(n // 4, lambda j: scatter(kept(0, 2 * j), kept(0, 2 * j + 1)))

    def reduce_step(k, c):
        count = n >> (k + 1)

        def send(i):
            h = lax.rem(z // (2 << k) + i + count // 2, count)
            t = other(k, h)
            zsend[t, c] = total(t, k, c).astype(BF16)
            z_copy(k, h, c).start()

        loop(count, send)

    for c in range(parts):
        reduce_step(0, c)

    rows[...] = jnp.zeros_like(rows)

    def turn(k):
        psf_t[span(k, pixels), 0:bins] = psf_ref[k].T
        psf_t[span(k, pixels), bins:2 * bins] = psf_ref[k + fold].T

    loop(fold, turn, unroll=True)

    def mark_t(i):
        size = 128
        lane = lax.broadcasted_iota(jnp.int32, (size, slots), 1)
        slot = cols[span(i, size), 1:2]
        onehot_t[span(i, size), :] = jnp.where(lane == slot, 1.0, 0.0).astype(BF16)

    loop(entries // 128, mark_t, unroll=True)

    for k in range(1, steps):
        for c in range(parts):
            reduce_step(k, c)
    for load in loads:
        load.wait()

    def pass_on(t, k, c):
        for j in reversed(range(k)):
            g_copy(j, t // (2 << j), c).start()
        p_copy(t, c).start()

    for c in range(parts):
        at = pl.ds(c * sub, sub)
        out = bad[at, :].astype(F32) * (total(z, steps, c) - obs[at, :].astype(F32))
        resid[z, my_rows(c), :] = out.astype(BF16)
        pass_on(z, steps, c)

    def gathered(h, where):
        pair = jnp.concatenate([resid[2 * h, where, :], resid[2 * h + 1, where, :]], axis=1)

        def block(i):
            at = span(i, step_rows)
            got = dot(onehot_t[at, where], pair)
            tile = jnp.broadcast_to(cols[at, 0:1], (step_rows, pixels))
            value = jnp.where(tile == 2 * h, got[:, 0:pixels], 0.0)
            value = jnp.where(tile == 2 * h + 1, got[:, pixels:2 * pixels], value)
            rows[at, :] = rows[at, :] + value

        loop(entries // step_rows, block, unroll=True)

    for k in reversed(range(1, steps)):
        count = n >> (k + 1)
        for c in range(parts):
            def arrive(i):
                h = lax.rem(z // (2 << k) + i, count)
                g_copy(k, h, c).wait_recv()
                pass_on(other(k, h), k, c)

            loop(count, arrive)

    def last(i):
        h = lax.rem(z // 2 + i, n // 2)
        for c in range(parts):
            g_copy(0, h, c).wait_recv()
            p_copy(other(0, h), c).start()
            gathered(h, my_rows(c))
        for c in range(parts):
            p_copy(2 * h, c, arriving=True).wait_recv()
            p_copy(2 * h + 1, c, arriving=True).wait_recv()
            gathered(h, peer_rows(c))

    loop(n // 2, last)

    def backward(i):
        at = span(i, step_rows)
        col = cols[at, :]
        kind = jnp.broadcast_to(col[:, 4:5], (step_rows, pixels))
        term = through(rows[at, :], kind, psf_t)
        block = jnp.broadcast_to(col[:, 3:4], (step_rows, bins))
        terms[at, :] = spread(term, block, blocks)

    loop(entries // step_rows, backward, unroll=True)

    share = sources // nd

    wing = wide // 2

    def summed(to, w):
        row = lax.broadcasted_iota(jnp.int32, (share, entries), 0) + to * share
        member = jnp.where(row == src_ref[...], 1.0, 0.0).astype(BF16)
        return dot(member, terms[:, w * wing:(w + 1) * wing])

    def d_copy(k, w):
        to = lax.rem(d + k, nd)
        return copy(
            dsend.at[k - 1, w], drecv.at[k - 1, w], ds_sem.at[k - 1, w], dr_sem.at[k - 1, w],
            {"dither": to},
        )

    for k in range(1, nd):
        for w in range(2):
            dsend[k - 1, w] = summed(lax.rem(d + k, nd), w).astype(BF16)
            d_copy(k, w).start()
    for w in range(2):
        grad_ref[:, w * wing:(w + 1) * wing] = summed(d, w)
    res_ref[...] = resid[z]
    for w in range(2):
        value = grad_ref[:, w * wing:(w + 1) * wing]
        for k in range(1, nd):
            d_copy(k, w).wait_recv()
            value = value + drecv[k - 1, w].astype(F32)
        grad_ref[:, w * wing:(w + 1) * wing] = value

    for k in range(1, nd):
        for w in range(2):
            d_copy(k, w).wait_send()
    for c in range(parts):
        loop(n, lambda t: f_copy(t, c).wait_send())
        loop(n, lambda t: p_copy(t, c).wait_send())
        for k in range(steps):
            loop(n >> (k + 1), lambda h: z_copy(k, h, c).wait_send())
            loop(n >> (k + 1), lambda h: g_copy(k, h, c).wait_send())


def place(grad_from, res_from, grad_to, res_to, sems):
    moves = [
        pltpu.make_async_copy(grad_from, grad_to, sems.at[0]),
        pltpu.make_async_copy(res_from, res_to, sems.at[1]),
    ]
    for move in moves:
        move.start()
    for move in moves:
        move.wait()


def per_device(
    n, nd, spectra, psf_blocks, observed, bad_mask,
    trace_tile, trace_slot, trace_source, trace_block, psf_index,
):
    entries = trace_slot.shape[0]
    slots, pixels = observed.shape[1:]
    kinds, bins, _ = psf_blocks.shape
    sources, wide = spectra.shape
    half = slots // 2
    steps = n.bit_length() - 1
    parts = 2
    sub = half // parts
    row = lambda a: a.reshape(1, entries)
    dma = pltpu.SemaphoreType.DMA
    grad, res = pl.pallas_call(
        functools.partial(kernel, (n, nd, steps, parts)),
        out_shape=(
            jax.ShapeDtypeStruct((sources // nd, wide), F32),
            jax.ShapeDtypeStruct((slots, pixels), BF16),
        ),
        in_specs=(
            [pl.BlockSpec(memory_space=pltpu.VMEM)] * 2
            + [pl.BlockSpec(memory_space=pl.ANY)] * 2
            + [pl.BlockSpec(memory_space=pltpu.VMEM)] * 5
        ),
        out_specs=[pl.BlockSpec(memory_space=pltpu.VMEM)] * 2,
        scratch_shapes=[
            pltpu.VMEM((entries, 8), jnp.int32),
            pltpu.VMEM((entries, pixels), BF16),
            pltpu.VMEM((entries, 2 * pixels), BF16),
            pltpu.VMEM((slots, entries), BF16),
            pltpu.VMEM((entries, slots), BF16),
            pltpu.VMEM((kinds // 2 * bins, 2 * pixels), BF16),
            pltpu.VMEM((kinds // 2 * pixels, 2 * bins), BF16),
            pltpu.VMEM((n, parts, sub, pixels), F32),
            pltpu.VMEM((n, parts, sub, pixels), BF16),
            pltpu.VMEM((n, parts, sub, pixels), BF16),
            pltpu.VMEM((steps, n // 2, parts, sub, pixels), BF16),
            pltpu.VMEM((n, parts, sub, pixels), BF16),
            pltpu.VMEM((n, slots, pixels), BF16),
            pltpu.VMEM((entries, pixels), F32),
            pltpu.VMEM((entries, wide), BF16),
            pltpu.VMEM((nd - 1, 2, sources // nd, wide // 2), BF16),
            pltpu.VMEM((nd - 1, 2, sources // nd, wide // 2), BF16),
            pltpu.VMEM((half, pixels), BF16),
            pltpu.VMEM((half, pixels), jnp.int32),
            dma((n, parts)), dma((n, parts)),
            dma((n, parts)), dma((steps, n // 2, parts)),
            dma((steps, n // 2, parts)), dma((steps, n // 2, parts)),
            dma((n, parts)), dma((n, parts)),
            dma((nd - 1, 2)), dma((nd - 1, 2)), dma((2,)),
        ],
        compiler_params=pltpu.CompilerParams(
            collective_id=0, has_side_effects=True, vmem_limit_bytes=56 * 1024 * 1024
        ),
        cost_estimate=pl.CostEstimate(
            flops=2 * entries * pixels * (2 * kinds * bins + 2 * n * slots + 8 * sources),
            bytes_accessed=2 * 1024 * 1024,
            transcendentals=0,
        ),
    )(
        spectra, psf_blocks, observed[0], bad_mask[0],
        row(trace_tile), row(trace_slot), row(trace_source), row(trace_block), row(psf_index),
    )
    grad, res = pl.pallas_call(
        place,
        out_shape=(
            jax.ShapeDtypeStruct(grad.shape, F32), jax.ShapeDtypeStruct(res.shape, BF16)
        ),
        in_specs=[pl.BlockSpec(memory_space=pl.ANY)] * 2,
        out_specs=[pl.BlockSpec(memory_space=pl.ANY)] * 2,
        scratch_shapes=[dma((2,))],
        compiler_params=pltpu.CompilerParams(vmem_limit_bytes=60 * 1024 * 1024),
    )(grad, res)
    return grad, res[None]


def solution(mesh):
    in_specs = (
        P(("groups", "tile"), "band"),
        P(),
        P(("groups", "dither"), "tile", None),
        P(("groups", "dither"), "tile", None),
        P(("groups", "tile", "dither", "band"), None),
        P(("groups", "tile", "dither", "band")),
        P(("groups", "tile", "dither", "band"), None),
        P(("groups", "tile", "dither", "band")),
        P(("groups", "tile", "dither", "band")),
    )
    out_specs = (P(("groups", "tile", "dither"), "band"), P(("groups", "dither"), "tile", None))
    fn = functools.partial(per_device, mesh.shape["tile"], mesh.shape["dither"])
    return jax.shard_map(fn, mesh=mesh, in_specs=in_specs, out_specs=out_specs, check_vma=False)
```

```python
import functools

import jax
import jax.numpy as jnp
from jax import lax
from jax.experimental import pallas as pl
from jax.experimental.pallas import tpu as pltpu
from jax.sharding import PartitionSpec as P

MESH = pl.DeviceIdType.MESH
F32, BF16 = jnp.float32, jnp.bfloat16


def dot(a, b):
    return jnp.dot(a, b, preferred_element_type=F32)


def kernel(
    cfg,
    spectra_ref, psf_ref, obs_ref, bad_ref, tile_ref, slot_ref, src_ref, blk_ref, kind_ref,
    grad_ref, res_ref,
    cols, traces, masked, onehot, onehot_t, psf_f, psf_t, own, fsend, frecv, zrecv, zsend,
    resid, rows, terms, dsend, drecv, obs, bad,
    fs_sem, fr_sem, zs_sem, zr_sem, gs_sem, gr_sem, ps_sem, pr_sem, ds_sem, dr_sem, in_sem,
):
    n, nd, steps, parts = cfg
    entries = tile_ref.shape[1]
    slots = obs_ref.shape[0]
    half = slots // 2
    sub = half // parts
    kinds, bins, pixels = psf_ref.shape
    sources, wide = spectra_ref.shape
    blocks = wide // bins
    fold = kinds // 2
    step_rows = min(256, entries, sub)
    z = lax.axis_index("tile")
    b = lax.axis_index("band")
    d = lax.axis_index("dither")
    peer = {"band": 1 - b}

    def bit(k):
        return lax.rem(z // (1 << k), 2)

    def partner(k):
        return {"tile": z + (1 - 2 * bit(k)) * (1 << k)}

    def kept(k, h):
        return h * (2 << k) + lax.rem(z, 2 << k)

    def other(k, h):
        return h * (2 << k) + (1 - bit(k)) * (1 << k) + lax.rem(z, 1 << k)

    barrier = pltpu.get_barrier_semaphore()

    def greet(where):
        pl.semaphore_signal(barrier, inc=1, device_id=where, device_id_type=MESH)

    greet(peer)
    for k in range(steps):
        greet(partner(k))
    for k in range(1, nd):
        greet({"dither": lax.rem(d + k, nd)})

    def loop(count, act, unroll=False):
        def body(s, _):
            act(s)
            return _

        lax.fori_loop(0, count, body, 0, unroll=unroll)

    def span(i, size, base=0):
        return pl.ds(pl.multiple_of(base + i * size, size), size)

    mine, theirs = span(b, half), span(1 - b, half)
    loads = [
        pltpu.make_async_copy(obs_ref.at[mine], obs, in_sem.at[0]),
        pltpu.make_async_copy(bad_ref.at[mine], bad, in_sem.at[1]),
    ]
    for load in loads:
        load.start()

    stack = [tile_ref[...], slot_ref[...], src_ref[...], blk_ref[...], kind_ref[...]]
    cols[...] = jnp.concatenate(stack + [kind_ref[...]] * 3, axis=0).T

    def spread(values, which, count):
        return jnp.concatenate(
            [jnp.where(which == k, values, 0.0).astype(BF16) for k in range(count)], axis=1
        )

    def through(values, kind, table):
        low = kind < fold
        product = dot(spread(values, jnp.where(low, kind, kind - fold), fold), table[...])
        width = product.shape[1] // 2
        return jnp.where(low, product[:, :width], product[:, width:])

    flat = psf_ref[...].reshape(kinds * bins, pixels)
    psf_f[:, 0:pixels] = flat[:fold * bins]
    psf_f[:, pixels:2 * pixels] = flat[fold * bins:]

    def forward(i):
        at = span(i, step_rows)
        col = cols[at, :]
        lane = lax.broadcasted_iota(jnp.int32, (step_rows, sources), 1)
        pick = jnp.where(lane == col[:, 2:3], 1.0, 0.0).astype(BF16)
        found = dot(pick, spectra_ref[...])
        block = jnp.broadcast_to(col[:, 3:4], (step_rows, bins))
        value = jnp.zeros((step_rows, bins), F32)
        for k in range(blocks):
            value = jnp.where(block == k, found[:, k * bins:(k + 1) * bins], value)
        kind = jnp.broadcast_to(col[:, 4:5], (step_rows, bins))
        traces[at, :] = through(value, kind, psf_f).astype(BF16)

    loop(entries // step_rows, forward, unroll=True)

    def mark(i):
        size = 128
        row = lax.broadcasted_iota(jnp.int32, (size, entries), 0) + i * size
        onehot[span(i, size), :] = jnp.where(row == slot_ref[...], 1.0, 0.0).astype(BF16)

    loop(slots // 128, mark, unroll=True)

    pl.semaphore_wait(barrier, 1 + steps + nd - 1)

    def my_rows(c):
        return span(c, sub, b * half)

    def peer_rows(c):
        return span(c, sub, (1 - b) * half)

    def copy(src, dst, send, recv, where):
        return pltpu.make_async_remote_copy(
            src_ref=src, dst_ref=dst, send_sem=send, recv_sem=recv,
            device_id=where, device_id_type=MESH,
        )

    def f_copy(t, c):
        return copy(fsend.at[t, c], frecv.at[t, c], fs_sem.at[t, c], fr_sem.at[t, c], peer)

    def z_copy(k, h, c):
        t = other(k, h)
        return copy(
            zsend.at[t, c], zrecv.at[k, h, c], zs_sem.at[t, c], zr_sem.at[k, h, c], partner(k)
        )

    def g_copy(k, h, c):
        block = resid.at[kept(k, h), my_rows(c)]
        return copy(block, block, gs_sem.at[k, h, c], gr_sem.at[k, h, c], partner(k))

    def p_copy(t, c, arriving=False):
        block = resid.at[t, peer_rows(c) if arriving else my_rows(c)]
        return copy(block, block, ps_sem.at[t, c], pr_sem.at[t, c], peer)

    def scatter(t, u):
        tile = jnp.broadcast_to(cols[:, 0:1], (entries, pixels))
        trace = traces[...].astype(F32)
        masked[:, 0:pixels] = jnp.where(tile == t, trace, 0.0).astype(BF16)
        masked[:, pixels:2 * pixels] = jnp.where(tile == u, trace, 0.0).astype(BF16)

        part = dot(onehot[theirs, :], masked[...]).astype(BF16)
        fsend[t] = part[:, 0:pixels].reshape(parts, sub, pixels)
        fsend[u] = part[:, pixels:2 * pixels].reshape(parts, sub, pixels)
        for c in range(parts):
            f_copy(t, c).start()
            f_copy(u, c).start()
        part = dot(onehot[mine, :], masked[...])
        own[t] = part[:, 0:pixels].reshape(parts, sub, pixels)
        own[u] = part[:, pixels:2 * pixels].reshape(parts, sub, pixels)

    def total(t, k, c):
        f_copy(t, c).wait_recv()
        value = own[t, c] + frecv[t, c].astype(F32)
        for j in range(k):
            z_copy(j, t // (2 << j), c).wait_recv()
            value = value + zrecv[j, t // (2 << j), c].astype(F32)
        return value

    loop(n // 4, lambda j: scatter(other(0, 2 * j), other(0, 2 * j + 1)))
    loop(n // 4, lambda j: scatter(kept(0, 2 * j), kept(0, 2 * j + 1)))

    def reduce_step(k, c):
        count = n >> (k + 1)

        def send(i):
            h = lax.rem(z // (2 << k) + i + count // 2, count)
            t = other(k, h)
            zsend[t, c] = total(t, k, c).astype(BF16)
            z_copy(k, h, c).start()

        loop(count, send)

    for c in range(parts):
        reduce_step(0, c)

    rows[...] = jnp.zeros_like(rows)

    def turn(k):
        psf_t[span(k, pixels), 0:bins] = psf_ref[k].T
        psf_t[span(k, pixels), bins:2 * bins] = psf_ref[k + fold].T

    loop(fold, turn, unroll=True)

    def mark_t(i):
        size = 128
        lane = lax.broadcasted_iota(jnp.int32, (size, slots), 1)
        slot = cols[span(i, size), 1:2]
        onehot_t[span(i, size), :] = jnp.where(lane == slot, 1.0, 0.0).astype(BF16)

    loop(entries // 128, mark_t, unroll=True)

    for k in range(1, steps):
        for c in range(parts):
            reduce_step(k, c)
    for load in loads:
        load.wait()

    def pass_on(t, k, c):
        for j in reversed(range(k)):
            g_copy(j, t // (2 << j), c).start()
        p_copy(t, c).start()

    for c in range(parts):
        at = pl.ds(c * sub, sub)
        out = bad[at, :].astype(F32) * (total(z, steps, c) - obs[at, :].astype(F32))
        resid[z, my_rows(c), :] = out.astype(BF16)
        pass_on(z, steps, c)

    def gathered(h, where):
        pair = jnp.concatenate([resid[2 * h, where, :], resid[2 * h + 1, where, :]], axis=1)

        def block(i):
            at = span(i, entries // 2)
            got = dot(onehot_t[at, where], pair)
            tile = jnp.broadcast_to(cols[at, 0:1], (entries // 2, pixels))
            value = jnp.where(tile == 2 * h, got[:, 0:pixels], 0.0)
            value = jnp.where(tile == 2 * h + 1, got[:, pixels:2 * pixels], value)
            rows[at, :] = rows[at, :] + value

        loop(2, block, unroll=True)

    for k in reversed(range(1, steps)):
        count = n >> (k + 1)
        for c in range(parts):
            def arrive(i):
                h = lax.rem(z // (2 << k) + i, count)
                g_copy(k, h, c).wait_recv()
                pass_on(other(k, h), k, c)

            loop(count, arrive)

    def last(i):
        h = lax.rem(z // 2 + i, n // 2)
        for c in range(parts):
            g_copy(0, h, c).wait_recv()
            p_copy(other(0, h), c).start()
            gathered(h, my_rows(c))
        for c in range(parts):
            p_copy(2 * h, c, arriving=True).wait_recv()
            p_copy(2 * h + 1, c, arriving=True).wait_recv()
            gathered(h, peer_rows(c))

    loop(n // 2, last)

    def backward(i):
        at = span(i, step_rows)
        col = cols[at, :]
        kind = jnp.broadcast_to(col[:, 4:5], (step_rows, pixels))
        term = through(rows[at, :], kind, psf_t)
        block = jnp.broadcast_to(col[:, 3:4], (step_rows, bins))
        terms[at, :] = spread(term, block, blocks)

    loop(entries // step_rows, backward, unroll=True)

    share = sources // nd

    wing = wide // 2

    def summed(to, w):
        row = lax.broadcasted_iota(jnp.int32, (share, entries), 0) + to * share
        member = jnp.where(row == src_ref[...], 1.0, 0.0).astype(BF16)
        return dot(member, terms[:, w * wing:(w + 1) * wing])

    def d_copy(k, w):
        to = lax.rem(d + k, nd)
        return copy(
            dsend.at[k - 1, w], drecv.at[k - 1, w], ds_sem.at[k - 1, w], dr_sem.at[k - 1, w],
            {"dither": to},
        )

    for k in range(1, nd):
        for w in range(2):
            dsend[k - 1, w] = summed(lax.rem(d + k, nd), w).astype(BF16)
            d_copy(k, w).start()
    for w in range(2):
        grad_ref[:, w * wing:(w + 1) * wing] = summed(d, w)
    res_ref[...] = resid[z]
    for w in range(2):
        value = grad_ref[:, w * wing:(w + 1) * wing]
        for k in range(1, nd):
            d_copy(k, w).wait_recv()
            value = value + drecv[k - 1, w].astype(F32)
        grad_ref[:, w * wing:(w + 1) * wing] = value

    for k in range(1, nd):
        for w in range(2):
            d_copy(k, w).wait_send()
    for c in range(parts):
        loop(n, lambda t: f_copy(t, c).wait_send())
        loop(n, lambda t: p_copy(t, c).wait_send())
        for k in range(steps):
            loop(n >> (k + 1), lambda h: z_copy(k, h, c).wait_send())
            loop(n >> (k + 1), lambda h: g_copy(k, h, c).wait_send())


def place(grad_from, res_from, grad_to, res_to):
    grad_to[...] = grad_from[...]
    res_to[...] = res_from[...]


def per_device(
    n, nd, spectra, psf_blocks, observed, bad_mask,
    trace_tile, trace_slot, trace_source, trace_block, psf_index,
):
    entries = trace_slot.shape[0]
    slots, pixels = observed.shape[1:]
    kinds, bins, _ = psf_blocks.shape
    sources, wide = spectra.shape
    half = slots // 2
    steps = n.bit_length() - 1
    parts = 2
    sub = half // parts
    row = lambda a: a.reshape(1, entries)
    dma = pltpu.SemaphoreType.DMA
    grad, res = pl.pallas_call(
        functools.partial(kernel, (n, nd, steps, parts)),
        out_shape=(
            jax.ShapeDtypeStruct((sources // nd, wide), F32),
            jax.ShapeDtypeStruct((slots, pixels), BF16),
        ),
        in_specs=(
            [pl.BlockSpec(memory_space=pltpu.VMEM)] * 2
            + [pl.BlockSpec(memory_space=pltpu.HBM)] * 2
            + [pl.BlockSpec(memory_space=pltpu.VMEM)] * 5
        ),
        out_specs=[pl.BlockSpec(memory_space=pltpu.VMEM)] * 2,
        scratch_shapes=[
            pltpu.VMEM((entries, 8), jnp.int32),
            pltpu.VMEM((entries, pixels), BF16),
            pltpu.VMEM((entries, 2 * pixels), BF16),
            pltpu.VMEM((slots, entries), BF16),
            pltpu.VMEM((entries, slots), BF16),
            pltpu.VMEM((kinds // 2 * bins, 2 * pixels), BF16),
            pltpu.VMEM((kinds // 2 * pixels, 2 * bins), BF16),
            pltpu.VMEM((n, parts, sub, pixels), F32),
            pltpu.VMEM((n, parts, sub, pixels), BF16),
            pltpu.VMEM((n, parts, sub, pixels), BF16),
            pltpu.VMEM((steps, n // 2, parts, sub, pixels), BF16),
            pltpu.VMEM((n, parts, sub, pixels), BF16),
            pltpu.VMEM((n, slots, pixels), BF16),
            pltpu.VMEM((entries, pixels), F32),
            pltpu.VMEM((entries, wide), BF16),
            pltpu.VMEM((nd - 1, 2, sources // nd, wide // 2), BF16),
            pltpu.VMEM((nd - 1, 2, sources // nd, wide // 2), BF16),
            pltpu.VMEM((half, pixels), BF16),
            pltpu.VMEM((half, pixels), jnp.int32),
            dma((n, parts)), dma((n, parts)),
            dma((n, parts)), dma((steps, n // 2, parts)),
            dma((steps, n // 2, parts)), dma((steps, n // 2, parts)),
            dma((n, parts)), dma((n, parts)),
            dma((nd - 1, 2)), dma((nd - 1, 2)), dma((2,)),
        ],
        compiler_params=pltpu.CompilerParams(
            collective_id=0, has_side_effects=True, vmem_limit_bytes=56 * 1024 * 1024
        ),
        cost_estimate=pl.CostEstimate(
            flops=2 * entries * pixels * (2 * kinds * bins + 2 * n * slots + 8 * sources),
            bytes_accessed=2 * 1024 * 1024,
            transcendentals=0,
        ),
    )(
        spectra, psf_blocks, observed[0], bad_mask[0],
        row(trace_tile), row(trace_slot), row(trace_source), row(trace_block), row(psf_index),
    )
    grad, res = pl.pallas_call(
        place,
        out_shape=(
            jax.ShapeDtypeStruct(grad.shape, F32), jax.ShapeDtypeStruct(res.shape, BF16)
        ),
        in_specs=[pl.BlockSpec(memory_space=pltpu.VMEM)] * 2,
        out_specs=[pl.BlockSpec(memory_space=pltpu.VMEM)] * 2,
    )(grad, res)
    return grad, res[None]


def solution(mesh):
    in_specs = (
        P(("groups", "tile"), "band"),
        P(),
        P(("groups", "dither"), "tile", None),
        P(("groups", "dither"), "tile", None),
        P(("groups", "tile", "dither", "band"), None),
        P(("groups", "tile", "dither", "band")),
        P(("groups", "tile", "dither", "band"), None),
        P(("groups", "tile", "dither", "band")),
        P(("groups", "tile", "dither", "band")),
    )
    out_specs = (P(("groups", "tile", "dither"), "band"), P(("groups", "dither"), "tile", None))
    fn = functools.partial(per_device, mesh.shape["tile"], mesh.shape["dither"])
    return jax.shard_map(fn, mesh=mesh, in_specs=in_specs, out_specs=out_specs, check_vma=False)
```

```python
import functools

import jax
import jax.numpy as jnp
from jax import lax
from jax.experimental import pallas as pl
from jax.experimental.pallas import tpu as pltpu
from jax.sharding import PartitionSpec as P

MESH = pl.DeviceIdType.MESH
F32, BF16 = jnp.float32, jnp.bfloat16


def dot(a, b):
    return jnp.dot(a, b, preferred_element_type=F32)


def kernel(
    cfg,
    spectra_ref, psf_ref, obs_ref, bad_ref, tile_ref, slot_ref, src_ref, blk_ref, kind_ref,
    grad_ref, res_ref,
    cols, traces, masked, onehot, onehot_t, psf_f, psf_t, own, fsend, frecv, zrecv, zsend,
    resid, rows, terms, dsend, drecv, obs, bad,
    fs_sem, fr_sem, zs_sem, zr_sem, gs_sem, gr_sem, ps_sem, pr_sem, ds_sem, dr_sem, in_sem,
):
    n, nd, steps, parts = cfg
    entries = tile_ref.shape[1]
    slots = obs_ref.shape[0]
    half = slots // 2
    sub = half // parts
    kinds, bins, pixels = psf_ref.shape
    sources, wide = spectra_ref.shape
    blocks = wide // bins
    fold = kinds // 2
    step_rows = min(256, entries)
    z = lax.axis_index("tile")
    b = lax.axis_index("band")
    d = lax.axis_index("dither")
    peer = {"band": 1 - b}

    def bit(k):
        return lax.rem(z // (1 << k), 2)

    def partner(k):
        return {"tile": z + (1 - 2 * bit(k)) * (1 << k)}

    def kept(k, h):
        return h * (2 << k) + lax.rem(z, 2 << k)

    def other(k, h):
        return h * (2 << k) + (1 - bit(k)) * (1 << k) + lax.rem(z, 1 << k)

    barrier = pltpu.get_barrier_semaphore()

    def greet(where):
        pl.semaphore_signal(barrier, inc=1, device_id=where, device_id_type=MESH)

    greet(peer)
    for k in range(steps):
        greet(partner(k))
    for k in range(1, nd):
        greet({"dither": lax.rem(d + k, nd)})

    def loop(count, act, unroll=False):
        def body(s, _):
            act(s)
            return _

        lax.fori_loop(0, count, body, 0, unroll=unroll)

    def span(i, size, base=0):
        return pl.ds(pl.multiple_of(base + i * size, size), size)

    mine, theirs = span(b, half), span(1 - b, half)
    loads = [
        pltpu.make_async_copy(obs_ref.at[mine], obs, in_sem.at[0]),
        pltpu.make_async_copy(bad_ref.at[mine], bad, in_sem.at[1]),
    ]
    for load in loads:
        load.start()

    stack = [tile_ref[...], slot_ref[...], src_ref[...], blk_ref[...], kind_ref[...]]
    cols[...] = jnp.concatenate(stack + [kind_ref[...]] * 3, axis=0).T

    def spread(values, which, count):
        return jnp.concatenate(
            [jnp.where(which == k, values, 0.0).astype(BF16) for k in range(count)], axis=1
        )

    def through(values, kind, table):
        low = kind < fold
        product = dot(spread(values, jnp.where(low, kind, kind - fold), fold), table[...])
        width = product.shape[1] // 2
        return jnp.where(low, product[:, :width], product[:, width:])

    flat = psf_ref[...].reshape(kinds * bins, pixels)
    psf_f[:, 0:pixels] = flat[:fold * bins]
    psf_f[:, pixels:2 * pixels] = flat[fold * bins:]

    def forward(i):
        at = span(i, step_rows)
        col = cols[at, :]
        lane = lax.broadcasted_iota(jnp.int32, (step_rows, sources), 1)
        pick = jnp.where(lane == col[:, 2:3], 1.0, 0.0).astype(BF16)
        found = dot(pick, spectra_ref[...])
        block = jnp.broadcast_to(col[:, 3:4], (step_rows, bins))
        value = jnp.zeros((step_rows, bins), F32)
        for k in range(blocks):
            value = jnp.where(block == k, found[:, k * bins:(k + 1) * bins], value)
        kind = jnp.broadcast_to(col[:, 4:5], (step_rows, bins))
        traces[at, :] = through(value, kind, psf_f).astype(BF16)

    loop(entries // step_rows, forward, unroll=True)

    def mark(i):
        size = 128
        row = lax.broadcasted_iota(jnp.int32, (size, entries), 0) + i * size
        onehot[span(i, size), :] = jnp.where(row == slot_ref[...], 1.0, 0.0).astype(BF16)

    loop(slots // 128, mark, unroll=True)

    pl.semaphore_wait(barrier, 1 + steps + nd - 1)

    def my_rows(c):
        return span(c, sub, b * half)

    def peer_rows(c):
        return span(c, sub, (1 - b) * half)

    def copy(src, dst, send, recv, where):
        return pltpu.make_async_remote_copy(
            src_ref=src, dst_ref=dst, send_sem=send, recv_sem=recv,
            device_id=where, device_id_type=MESH,
        )

    def f_copy(t, c):
        return copy(fsend.at[t, c], frecv.at[t, c], fs_sem.at[t, c], fr_sem.at[t, c], peer)

    def z_copy(k, h, c):
        t = other(k, h)
        return copy(
            zsend.at[t, c], zrecv.at[k, h, c], zs_sem.at[t, c], zr_sem.at[k, h, c], partner(k)
        )

    def g_copy(k, h, c):
        block = resid.at[kept(k, h), my_rows(c)]
        return copy(block, block, gs_sem.at[k, h, c], gr_sem.at[k, h, c], partner(k))

    def p_copy(t, c, arriving=False):
        block = resid.at[t, peer_rows(c) if arriving else my_rows(c)]
        return copy(block, block, ps_sem.at[t, c], pr_sem.at[t, c], peer)

    def scatter(t, u):
        tile = jnp.broadcast_to(cols[:, 0:1], (entries, pixels))
        trace = traces[...].astype(F32)
        masked[:, 0:pixels] = jnp.where(tile == t, trace, 0.0).astype(BF16)
        masked[:, pixels:2 * pixels] = jnp.where(tile == u, trace, 0.0).astype(BF16)

        part = dot(onehot[theirs, :], masked[...]).astype(BF16)
        fsend[t] = part[:, 0:pixels].reshape(parts, sub, pixels)
        fsend[u] = part[:, pixels:2 * pixels].reshape(parts, sub, pixels)
        for c in range(parts):
            f_copy(t, c).start()
            f_copy(u, c).start()
        part = dot(onehot[mine, :], masked[...])
        own[t] = part[:, 0:pixels].reshape(parts, sub, pixels)
        own[u] = part[:, pixels:2 * pixels].reshape(parts, sub, pixels)

    def total(t, k, c):
        f_copy(t, c).wait_recv()
        value = own[t, c] + frecv[t, c].astype(F32)
        for j in range(k):
            z_copy(j, t // (2 << j), c).wait_recv()
            value = value + zrecv[j, t // (2 << j), c].astype(F32)
        return value

    loop(n // 4, lambda j: scatter(other(0, 2 * j), other(0, 2 * j + 1)))
    loop(n // 4, lambda j: scatter(kept(0, 2 * j), kept(0, 2 * j + 1)))

    def reduce_step(k, c):
        count = n >> (k + 1)

        def send(i):
            h = lax.rem(z // (2 << k) + i + count // 2, count)
            t = other(k, h)
            zsend[t, c] = total(t, k, c).astype(BF16)
            z_copy(k, h, c).start()

        loop(count, send)

    for c in range(parts):
        reduce_step(0, c)

    rows[...] = jnp.zeros_like(rows)

    def turn(k):
        psf_t[span(k, pixels), 0:bins] = psf_ref[k].T
        psf_t[span(k, pixels), bins:2 * bins] = psf_ref[k + fold].T

    loop(fold, turn, unroll=True)

    def mark_t(i):
        size = 128
        lane = lax.broadcasted_iota(jnp.int32, (size, slots), 1)
        slot = cols[span(i, size), 1:2]
        onehot_t[span(i, size), :] = jnp.where(lane == slot, 1.0, 0.0).astype(BF16)

    loop(entries // 128, mark_t, unroll=True)

    def pass_on(t, k, c):
        for j in reversed(range(k)):
            g_copy(j, t // (2 << j), c).start()
        p_copy(t, c).start()

    def finish(c):
        if c == 0:
            for load in loads:
                load.wait()
        at = pl.ds(c * sub, sub)
        out = bad[at, :].astype(F32) * (total(z, steps, c) - obs[at, :].astype(F32))
        resid[z, my_rows(c), :] = out.astype(BF16)
        pass_on(z, steps, c)

    def arrive_step(k, c):
        count = n >> (k + 1)

        def arrive(i):
            h = lax.rem(z // (2 << k) + i, count)
            g_copy(k, h, c).wait_recv()
            pass_on(other(k, h), k, c)

        loop(count, arrive)

    stages = [functools.partial(reduce_step, k) for k in range(1, steps)]
    stages += [finish] + [functools.partial(arrive_step, k) for k in reversed(range(1, steps))]
    for i in range(parts + len(stages) - 1):
        for j, stage in enumerate(stages):
            if 0 <= i - j < parts:
                stage(i - j)

    def gathered(h, where):
        pair = jnp.concatenate([resid[2 * h, where, :], resid[2 * h + 1, where, :]], axis=1)

        def block(i):
            at = span(i, entries // 2)
            got = dot(onehot_t[at, where], pair)
            tile = jnp.broadcast_to(cols[at, 0:1], (entries // 2, pixels))
            value = jnp.where(tile == 2 * h, got[:, 0:pixels], 0.0)
            value = jnp.where(tile == 2 * h + 1, got[:, pixels:2 * pixels], value)
            rows[at, :] = rows[at, :] + value

        loop(2, block, unroll=True)

    def last(i):
        h = lax.rem(z // 2 + i, n // 2)
        for c in range(parts):
            g_copy(0, h, c).wait_recv()
            p_copy(other(0, h), c).start()
            if c % 2:
                gathered(h, span(c // 2, 2 * sub, b * half))
        for c in range(parts):
            p_copy(2 * h, c, arriving=True).wait_recv()
            p_copy(2 * h + 1, c, arriving=True).wait_recv()
            if c % 2:
                gathered(h, span(c // 2, 2 * sub, (1 - b) * half))

    loop(n // 2, last)

    def backward(i):
        at = span(i, step_rows)
        col = cols[at, :]
        kind = jnp.broadcast_to(col[:, 4:5], (step_rows, pixels))
        term = through(rows[at, :], kind, psf_t)
        block = jnp.broadcast_to(col[:, 3:4], (step_rows, bins))
        terms[at, :] = spread(term, block, blocks)

    loop(entries // step_rows, backward, unroll=True)

    share = sources // nd

    wing = wide // 2

    def summed(to, w):
        row = lax.broadcasted_iota(jnp.int32, (share, entries), 0) + to * share
        member = jnp.where(row == src_ref[...], 1.0, 0.0).astype(BF16)
        return dot(member, terms[:, w * wing:(w + 1) * wing])

    def d_copy(k, w):
        to = lax.rem(d + k, nd)
        return copy(
            dsend.at[k - 1, w], drecv.at[k - 1, w], ds_sem.at[k - 1, w], dr_sem.at[k - 1, w],
            {"dither": to},
        )

    for k in range(1, nd):
        for w in range(2):
            dsend[k - 1, w] = summed(lax.rem(d + k, nd), w).astype(BF16)
            d_copy(k, w).start()
    for w in range(2):
        grad_ref[:, w * wing:(w + 1) * wing] = summed(d, w)
    res_ref[...] = resid[z]
    for w in range(2):
        value = grad_ref[:, w * wing:(w + 1) * wing]
        for k in range(1, nd):
            d_copy(k, w).wait_recv()
            value = value + drecv[k - 1, w].astype(F32)
        grad_ref[:, w * wing:(w + 1) * wing] = value

    for k in range(1, nd):
        for w in range(2):
            d_copy(k, w).wait_send()
    for c in range(parts):
        loop(n, lambda t: f_copy(t, c).wait_send())
        loop(n, lambda t: p_copy(t, c).wait_send())
        for k in range(steps):
            loop(n >> (k + 1), lambda h: z_copy(k, h, c).wait_send())
            loop(n >> (k + 1), lambda h: g_copy(k, h, c).wait_send())


def place(grad_from, res_from, grad_to, res_to):
    grad_to[...] = grad_from[...]
    res_to[...] = res_from[...]


def per_device(
    n, nd, spectra, psf_blocks, observed, bad_mask,
    trace_tile, trace_slot, trace_source, trace_block, psf_index,
):
    entries = trace_slot.shape[0]
    slots, pixels = observed.shape[1:]
    kinds, bins, _ = psf_blocks.shape
    sources, wide = spectra.shape
    half = slots // 2
    steps = n.bit_length() - 1
    parts = 4
    sub = half // parts
    row = lambda a: a.reshape(1, entries)
    dma = pltpu.SemaphoreType.DMA
    grad, res = pl.pallas_call(
        functools.partial(kernel, (n, nd, steps, parts)),
        out_shape=(
            jax.ShapeDtypeStruct((sources // nd, wide), F32),
            jax.ShapeDtypeStruct((slots, pixels), BF16),
        ),
        in_specs=(
            [pl.BlockSpec(memory_space=pltpu.VMEM)] * 2
            + [pl.BlockSpec(memory_space=pltpu.HBM)] * 2
            + [pl.BlockSpec(memory_space=pltpu.VMEM)] * 5
        ),
        out_specs=[pl.BlockSpec(memory_space=pltpu.VMEM)] * 2,
        scratch_shapes=[
            pltpu.VMEM((entries, 8), jnp.int32),
            pltpu.VMEM((entries, pixels), BF16),
            pltpu.VMEM((entries, 2 * pixels), BF16),
            pltpu.VMEM((slots, entries), BF16),
            pltpu.VMEM((entries, slots), BF16),
            pltpu.VMEM((kinds // 2 * bins, 2 * pixels), BF16),
            pltpu.VMEM((kinds // 2 * pixels, 2 * bins), BF16),
            pltpu.VMEM((n, parts, sub, pixels), F32),
            pltpu.VMEM((n, parts, sub, pixels), BF16),
            pltpu.VMEM((n, parts, sub, pixels), BF16),
            pltpu.VMEM((steps, n // 2, parts, sub, pixels), BF16),
            pltpu.VMEM((n, parts, sub, pixels), BF16),
            pltpu.VMEM((n, slots, pixels), BF16),
            pltpu.VMEM((entries, pixels), F32),
            pltpu.VMEM((entries, wide), BF16),
            pltpu.VMEM((nd - 1, 2, sources // nd, wide // 2), BF16),
            pltpu.VMEM((nd - 1, 2, sources // nd, wide // 2), BF16),
            pltpu.VMEM((half, pixels), BF16),
            pltpu.VMEM((half, pixels), jnp.int32),
            dma((n, parts)), dma((n, parts)),
            dma((n, parts)), dma((steps, n // 2, parts)),
            dma((steps, n // 2, parts)), dma((steps, n // 2, parts)),
            dma((n, parts)), dma((n, parts)),
            dma((nd - 1, 2)), dma((nd - 1, 2)), dma((2,)),
        ],
        compiler_params=pltpu.CompilerParams(
            collective_id=0, has_side_effects=True, vmem_limit_bytes=56 * 1024 * 1024
        ),
        cost_estimate=pl.CostEstimate(
            flops=2 * entries * pixels * (2 * kinds * bins + 2 * n * slots + 8 * sources),
            bytes_accessed=2 * 1024 * 1024,
            transcendentals=0,
        ),
    )(
        spectra, psf_blocks, observed[0], bad_mask[0],
        row(trace_tile), row(trace_slot), row(trace_source), row(trace_block), row(psf_index),
    )
    grad, res = pl.pallas_call(
        place,
        out_shape=(
            jax.ShapeDtypeStruct(grad.shape, F32), jax.ShapeDtypeStruct(res.shape, BF16)
        ),
        in_specs=[pl.BlockSpec(memory_space=pltpu.VMEM)] * 2,
        out_specs=[pl.BlockSpec(memory_space=pltpu.VMEM)] * 2,
    )(grad, res)
    return grad, res[None]


def solution(mesh):
    in_specs = (
        P(("groups", "tile"), "band"),
        P(),
        P(("groups", "dither"), "tile", None),
        P(("groups", "dither"), "tile", None),
        P(("groups", "tile", "dither", "band"), None),
        P(("groups", "tile", "dither", "band")),
        P(("groups", "tile", "dither", "band"), None),
        P(("groups", "tile", "dither", "band")),
        P(("groups", "tile", "dither", "band")),
    )
    out_specs = (P(("groups", "tile", "dither"), "band"), P(("groups", "dither"), "tile", None))
    fn = functools.partial(per_device, mesh.shape["tile"], mesh.shape["dither"])
    return jax.shard_map(fn, mesh=mesh, in_specs=in_specs, out_specs=out_specs, check_vma=False)
```

```python
import functools

import jax
import jax.numpy as jnp
from jax import lax
from jax.experimental import pallas as pl
from jax.experimental.pallas import tpu as pltpu
from jax.sharding import PartitionSpec as P

MESH = pl.DeviceIdType.MESH
F32, BF16 = jnp.float32, jnp.bfloat16


def dot(a, b):
    return jnp.dot(a, b, preferred_element_type=F32)


def kernel(
    cfg,
    spectra_ref, psf_ref, obs_ref, bad_ref, tile_ref, slot_ref, src_ref, blk_ref, kind_ref,
    grad_ref, res_ref,
    cols, traces, masked, onehot, onehot_t, psf_f, psf_t, own, fsend, frecv, zrecv, zsend,
    resid, rows, terms, dsend, drecv, obs, bad,
    fs_sem, fr_sem, zs_sem, zr_sem, gs_sem, gr_sem, ps_sem, pr_sem, ds_sem, dr_sem, in_sem,
):
    n, nd, steps, parts = cfg
    entries = tile_ref.shape[1]
    slots = obs_ref.shape[0]
    half = slots // 2
    sub = half // parts
    kinds, bins, pixels = psf_ref.shape
    sources, wide = spectra_ref.shape
    blocks = wide // bins
    fold = kinds // 2
    step_rows = min(256, entries)
    z = lax.axis_index("tile")
    b = lax.axis_index("band")
    d = lax.axis_index("dither")
    peer = {"band": 1 - b}

    def bit(k):
        return lax.rem(z // (1 << k), 2)

    def partner(k):
        return {"tile": z + (1 - 2 * bit(k)) * (1 << k)}

    def kept(k, h):
        return h * (2 << k) + lax.rem(z, 2 << k)

    def other(k, h):
        return h * (2 << k) + (1 - bit(k)) * (1 << k) + lax.rem(z, 1 << k)

    barrier = pltpu.get_barrier_semaphore()

    def greet(where):
        pl.semaphore_signal(barrier, inc=1, device_id=where, device_id_type=MESH)

    greet(peer)
    for k in range(steps):
        greet(partner(k))
    for k in range(1, nd):
        greet({"dither": lax.rem(d + k, nd)})

    def loop(count, act, unroll=False):
        def body(s, _):
            act(s)
            return _

        lax.fori_loop(0, count, body, 0, unroll=unroll)

    def span(i, size, base=0):
        return pl.ds(pl.multiple_of(base + i * size, size), size)

    mine, theirs = span(b, half), span(1 - b, half)
    loads = [
        pltpu.make_async_copy(obs_ref.at[mine], obs, in_sem.at[0]),
        pltpu.make_async_copy(bad_ref.at[mine], bad, in_sem.at[1]),
    ]
    for load in loads:
        load.start()

    stack = [tile_ref[...], slot_ref[...], src_ref[...], blk_ref[...], kind_ref[...]]
    cols[...] = jnp.concatenate(stack + [kind_ref[...]] * 3, axis=0).T

    def spread(values, which, count):
        return jnp.concatenate(
            [jnp.where(which == k, values, 0.0).astype(BF16) for k in range(count)], axis=1
        )

    def through(values, kind, table):
        low = kind < fold
        product = dot(spread(values, jnp.where(low, kind, kind - fold), fold), table[...])
        width = product.shape[1] // 2
        return jnp.where(low, product[:, :width], product[:, width:])

    flat = psf_ref[...].reshape(kinds * bins, pixels)
    psf_f[:, 0:pixels] = flat[:fold * bins]
    psf_f[:, pixels:2 * pixels] = flat[fold * bins:]

    def forward(i):
        at = span(i, step_rows)
        col = cols[at, :]
        lane = lax.broadcasted_iota(jnp.int32, (step_rows, sources), 1)
        pick = jnp.where(lane == col[:, 2:3], 1.0, 0.0).astype(BF16)
        found = dot(pick, spectra_ref[...])
        block = jnp.broadcast_to(col[:, 3:4], (step_rows, bins))
        value = jnp.zeros((step_rows, bins), F32)
        for k in range(blocks):
            value = jnp.where(block == k, found[:, k * bins:(k + 1) * bins], value)
        kind = jnp.broadcast_to(col[:, 4:5], (step_rows, bins))
        traces[at, :] = through(value, kind, psf_f).astype(BF16)

    loop(entries // step_rows, forward, unroll=True)

    def mark(i):
        size = 128
        row = lax.broadcasted_iota(jnp.int32, (size, entries), 0) + i * size
        onehot[span(i, size), :] = jnp.where(row == slot_ref[...], 1.0, 0.0).astype(BF16)

    loop(slots // 128, mark, unroll=True)

    pl.semaphore_wait(barrier, 1 + steps + nd - 1)

    def my_rows(c):
        return span(c, sub, b * half)

    def copy(src, dst, send, recv, where):
        return pltpu.make_async_remote_copy(
            src_ref=src, dst_ref=dst, send_sem=send, recv_sem=recv,
            device_id=where, device_id_type=MESH,
        )

    def f_copy(t):
        return copy(fsend.at[t], frecv.at[t], fs_sem.at[t], fr_sem.at[t], peer)

    def z_copy(k, h, c):
        t = other(k, h)
        return copy(
            zsend.at[t, c], zrecv.at[k, h, c], zs_sem.at[t, c], zr_sem.at[k, h, c], partner(k)
        )

    def g_copy(k, h, c):
        block = resid.at[kept(k, h), my_rows(c)]
        return copy(block, block, gs_sem.at[k, h, c], gr_sem.at[k, h, c], partner(k))

    def p_copy(t, arriving=False):
        block = resid.at[t, theirs if arriving else mine]
        return copy(block, block, ps_sem.at[t], pr_sem.at[t], peer)

    def scatter(t, u):
        tile = jnp.broadcast_to(cols[:, 0:1], (entries, pixels))
        trace = traces[...].astype(F32)
        masked[:, 0:pixels] = jnp.where(tile == t, trace, 0.0).astype(BF16)
        masked[:, pixels:2 * pixels] = jnp.where(tile == u, trace, 0.0).astype(BF16)

        part = dot(onehot[theirs, :], masked[...]).astype(BF16)
        fsend[t] = part[:, 0:pixels].reshape(parts, sub, pixels)
        fsend[u] = part[:, pixels:2 * pixels].reshape(parts, sub, pixels)
        f_copy(t).start()
        f_copy(u).start()
        part = dot(onehot[mine, :], masked[...])
        own[t] = part[:, 0:pixels].reshape(parts, sub, pixels)
        own[u] = part[:, pixels:2 * pixels].reshape(parts, sub, pixels)

    def total(t, k, c):
        if c == 0:
            f_copy(t).wait_recv()
        value = own[t, c] + frecv[t, c].astype(F32)
        for j in range(k):
            z_copy(j, t // (2 << j), c).wait_recv()
            value = value + zrecv[j, t // (2 << j), c].astype(F32)
        return value

    loop(n // 4, lambda j: scatter(other(0, 2 * j), other(0, 2 * j + 1)))
    loop(n // 4, lambda j: scatter(kept(0, 2 * j), kept(0, 2 * j + 1)))

    def reduce_step(k, c):
        count = n >> (k + 1)

        def send(i):
            h = lax.rem(z // (2 << k) + i + count // 2, count)
            t = other(k, h)
            zsend[t, c] = total(t, k, c).astype(BF16)
            z_copy(k, h, c).start()

        loop(count, send)

    for c in range(parts):
        reduce_step(0, c)

    rows[...] = jnp.zeros_like(rows)

    def turn(k):
        psf_t[span(k, pixels), 0:bins] = psf_ref[k].T
        psf_t[span(k, pixels), bins:2 * bins] = psf_ref[k + fold].T

    loop(fold, turn, unroll=True)

    def mark_t(i):
        size = 128
        lane = lax.broadcasted_iota(jnp.int32, (size, slots), 1)
        slot = cols[span(i, size), 1:2]
        onehot_t[span(i, size), :] = jnp.where(lane == slot, 1.0, 0.0).astype(BF16)

    loop(entries // 128, mark_t, unroll=True)

    def pass_on(t, k, c):
        for j in reversed(range(k)):
            g_copy(j, t // (2 << j), c).start()
        if c == parts - 1:
            p_copy(t).start()

    def finish(c):
        if c == 0:
            for load in loads:
                load.wait()
        at = pl.ds(c * sub, sub)
        out = bad[at, :].astype(F32) * (total(z, steps, c) - obs[at, :].astype(F32))
        resid[z, my_rows(c), :] = out.astype(BF16)
        pass_on(z, steps, c)

    def arrive_step(k, c):
        count = n >> (k + 1)

        def arrive(i):
            h = lax.rem(z // (2 << k) + i, count)
            g_copy(k, h, c).wait_recv()
            pass_on(other(k, h), k, c)

        loop(count, arrive)

    stages = [functools.partial(reduce_step, k) for k in range(1, steps)]
    stages += [finish] + [functools.partial(arrive_step, k) for k in reversed(range(1, steps))]
    for i in range(parts + len(stages) - 1):
        for j, stage in enumerate(stages):
            if 0 <= i - j < parts:
                stage(i - j)

    def gathered(h, where):
        pair = jnp.concatenate([resid[2 * h, where, :], resid[2 * h + 1, where, :]], axis=1)

        def block(i):
            at = span(i, entries // 2)
            got = dot(onehot_t[at, where], pair)
            tile = jnp.broadcast_to(cols[at, 0:1], (entries // 2, pixels))
            value = jnp.where(tile == 2 * h, got[:, 0:pixels], 0.0)
            value = jnp.where(tile == 2 * h + 1, got[:, pixels:2 * pixels], value)
            rows[at, :] = rows[at, :] + value

        loop(2, block, unroll=True)

    def last(i):
        h = lax.rem(z // 2 + i, n // 2)
        for c in range(parts):
            g_copy(0, h, c).wait_recv()
        p_copy(other(0, h)).start()
        gathered(h, mine)
        p_copy(2 * h, arriving=True).wait_recv()
        p_copy(2 * h + 1, arriving=True).wait_recv()
        gathered(h, theirs)

    loop(n // 2, last)

    def backward(i):
        at = span(i, step_rows)
        col = cols[at, :]
        kind = jnp.broadcast_to(col[:, 4:5], (step_rows, pixels))
        term = through(rows[at, :], kind, psf_t)
        block = jnp.broadcast_to(col[:, 3:4], (step_rows, bins))
        terms[at, :] = spread(term, block, blocks)

    loop(entries // step_rows, backward, unroll=True)

    share = sources // nd

    wing = wide // 2

    def summed(to, w):
        row = lax.broadcasted_iota(jnp.int32, (share, entries), 0) + to * share
        member = jnp.where(row == src_ref[...], 1.0, 0.0).astype(BF16)
        return dot(member, terms[:, w * wing:(w + 1) * wing])

    def d_copy(k, w):
        to = lax.rem(d + k, nd)
        return copy(
            dsend.at[k - 1, w], drecv.at[k - 1, w], ds_sem.at[k - 1, w], dr_sem.at[k - 1, w],
            {"dither": to},
        )

    for k in range(1, nd):
        for w in range(2):
            dsend[k - 1, w] = summed(lax.rem(d + k, nd), w).astype(BF16)
            d_copy(k, w).start()
    for w in range(2):
        grad_ref[:, w * wing:(w + 1) * wing] = summed(d, w)
    res_ref[...] = resid[z]
    for w in range(2):
        value = grad_ref[:, w * wing:(w + 1) * wing]
        for k in range(1, nd):
            d_copy(k, w).wait_recv()
            value = value + drecv[k - 1, w].astype(F32)
        grad_ref[:, w * wing:(w + 1) * wing] = value

    for k in range(1, nd):
        for w in range(2):
            d_copy(k, w).wait_send()
    loop(n, lambda t: f_copy(t).wait_send())
    loop(n, lambda t: p_copy(t).wait_send())
    for c in range(parts):
        for k in range(steps):
            loop(n >> (k + 1), lambda h: z_copy(k, h, c).wait_send())
            loop(n >> (k + 1), lambda h: g_copy(k, h, c).wait_send())


def place(grad_from, res_from, grad_to, res_to):
    grad_to[...] = grad_from[...]
    res_to[...] = res_from[...]


def per_device(
    n, nd, spectra, psf_blocks, observed, bad_mask,
    trace_tile, trace_slot, trace_source, trace_block, psf_index,
):
    entries = trace_slot.shape[0]
    slots, pixels = observed.shape[1:]
    kinds, bins, _ = psf_blocks.shape
    sources, wide = spectra.shape
    half = slots // 2
    steps = n.bit_length() - 1
    parts = 2
    sub = half // parts
    row = lambda a: a.reshape(1, entries)
    dma = pltpu.SemaphoreType.DMA
    grad, res = pl.pallas_call(
        functools.partial(kernel, (n, nd, steps, parts)),
        out_shape=(
            jax.ShapeDtypeStruct((sources // nd, wide), F32),
            jax.ShapeDtypeStruct((slots, pixels), BF16),
        ),
        in_specs=(
            [pl.BlockSpec(memory_space=pltpu.VMEM)] * 2
            + [pl.BlockSpec(memory_space=pltpu.HBM)] * 2
            + [pl.BlockSpec(memory_space=pltpu.VMEM)] * 5
        ),
        out_specs=[pl.BlockSpec(memory_space=pltpu.VMEM)] * 2,
        scratch_shapes=[
            pltpu.VMEM((entries, 8), jnp.int32),
            pltpu.VMEM((entries, pixels), BF16),
            pltpu.VMEM((entries, 2 * pixels), BF16),
            pltpu.VMEM((slots, entries), BF16),
            pltpu.VMEM((entries, slots), BF16),
            pltpu.VMEM((kinds // 2 * bins, 2 * pixels), BF16),
            pltpu.VMEM((kinds // 2 * pixels, 2 * bins), BF16),
            pltpu.VMEM((n, parts, sub, pixels), F32),
            pltpu.VMEM((n, parts, sub, pixels), BF16),
            pltpu.VMEM((n, parts, sub, pixels), BF16),
            pltpu.VMEM((steps, n // 2, parts, sub, pixels), BF16),
            pltpu.VMEM((n, parts, sub, pixels), BF16),
            pltpu.VMEM((n, slots, pixels), BF16),
            pltpu.VMEM((entries, pixels), F32),
            pltpu.VMEM((entries, wide), BF16),
            pltpu.VMEM((nd - 1, 2, sources // nd, wide // 2), BF16),
            pltpu.VMEM((nd - 1, 2, sources // nd, wide // 2), BF16),
            pltpu.VMEM((half, pixels), BF16),
            pltpu.VMEM((half, pixels), jnp.int32),
            dma((n,)), dma((n,)),
            dma((n, parts)), dma((steps, n // 2, parts)),
            dma((steps, n // 2, parts)), dma((steps, n // 2, parts)),
            dma((n,)), dma((n,)),
            dma((nd - 1, 2)), dma((nd - 1, 2)), dma((2,)),
        ],
        compiler_params=pltpu.CompilerParams(
            collective_id=0, has_side_effects=True, vmem_limit_bytes=56 * 1024 * 1024
        ),
        cost_estimate=pl.CostEstimate(
            flops=2 * entries * pixels * (2 * kinds * bins + 2 * n * slots + 8 * sources),
            bytes_accessed=2 * 1024 * 1024,
            transcendentals=0,
        ),
    )(
        spectra, psf_blocks, observed[0], bad_mask[0],
        row(trace_tile), row(trace_slot), row(trace_source), row(trace_block), row(psf_index),
    )
    grad, res = pl.pallas_call(
        place,
        out_shape=(
            jax.ShapeDtypeStruct(grad.shape, F32), jax.ShapeDtypeStruct(res.shape, BF16)
        ),
        in_specs=[pl.BlockSpec(memory_space=pltpu.VMEM)] * 2,
        out_specs=[pl.BlockSpec(memory_space=pltpu.VMEM)] * 2,
    )(grad, res)
    return grad, res[None]


def solution(mesh):
    in_specs = (
        P(("groups", "tile"), "band"),
        P(),
        P(("groups", "dither"), "tile", None),
        P(("groups", "dither"), "tile", None),
        P(("groups", "tile", "dither", "band"), None),
        P(("groups", "tile", "dither", "band")),
        P(("groups", "tile", "dither", "band"), None),
        P(("groups", "tile", "dither", "band")),
        P(("groups", "tile", "dither", "band")),
    )
    out_specs = (P(("groups", "tile", "dither"), "band"), P(("groups", "dither"), "tile", None))
    fn = functools.partial(per_device, mesh.shape["tile"], mesh.shape["dither"])
    return jax.shard_map(fn, mesh=mesh, in_specs=in_specs, out_specs=out_specs, check_vma=False)
```
